512 devices in a mesh: clip: 32 (over z_lo, x, core), layer: 16 (over y, z_hi).
Axes of the slice: x: 4, y: 4, z: 16 (z_hi: 4, z_lo: 4; z = z_hi * 4 + z_lo), core: 2. Of those that a mesh axis runs over, the one named last changes fastest.
Arguments:
- acts: bfloat16 [16, 8192, 5120], P('layer', 'clip'), may hold values from -6 to 6
- grads: bfloat16 [16, 8192, 5120], P('layer', 'clip'), may hold values from -6 to 6
- in_factor: bfloat16 [16, 5120, 64], P('layer'), may hold values from -0.078125 to 0.078125
- out_factor: bfloat16 [16, 5120, 64], P('layer'), may hold values from -0.078125 to 0.078125
- clip_tokens: int32 [1024], P('clip'), may hold values from 1 to 16, as said below
Outputs:
- similarity: float32 [1024, 1024], P('clip', 'layer')
The draws below stay inside these ranges and needn't reach their ends.
Inputs may be any that keep to these rules, and one draw needn't show every extreme that they name: `clip_tokens`: the clips of every block hold exactly 256 rows together, and some clip of every block has 16 rows.
All inputs are finite; a program needn't handle non-finite values.
Results may differ from the reference program's by a relative error of at most 0.0016.
Values may be sent and summed in bfloat16 or wider, within the bound.
A program may use at most 64 MiB of HBM per device.

```python
import math
import jax
import jax.numpy as jnp

D = 5120
KIN = 64
KOUT = 64
CLIPS_DEV = 32
MOST = 16
CAP = 256
LAYERS = 16
CLIPS = 1024
ROWS = 8192
N_CLIP = 32


def draw_clip_tokens(key, part):
    key = jax.random.fold_in(key, 11)
    first, second, third, fourth, fifth = jax.random.split(key, 5)
    blocks = CLIPS // CLIPS_DEV
    quads = CLIPS_DEV // 4
    half = MOST // 2
    delta = jax.random.randint(first, (blocks, quads, 2), 1 - half, half)
    base = jnp.stack([half + delta[..., 0], half - delta[..., 0], half + delta[..., 1], half - delta[..., 1]], axis=-1)
    left = jax.random.randint(second, (blocks,), 1, half)
    right = jax.random.randint(third, (blocks,), 1, half)
    special = jnp.stack([jnp.full((blocks,), MOST, jnp.int32), left, right, MOST - left - right], axis=-1)
    chosen = jax.random.randint(fourth, (blocks,), 0, quads)
    quad_index = jnp.arange(quads, dtype=jnp.int32)
    counts = jnp.where(quad_index[None, :, None] == chosen[:, None, None], special[:, None, :], base)
    counts = counts.reshape(blocks, CLIPS_DEV)
    block_keys = jax.random.split(fifth, blocks)
    orders = jax.vmap(lambda one_key: jax.random.permutation(one_key, CLIPS_DEV))(block_keys)
    counts = jnp.take_along_axis(counts, orders, axis=1)
    return counts.reshape(CLIPS).astype(jnp.int32)


def levels(own_key, extent, shards, least, top_value):
    def one(axis_at, blocks):
        heights = jax.random.uniform(jax.random.fold_in(jax.random.fold_in(own_key, 6), axis_at), (blocks,), jnp.float32, least / len(shards), top_value / len(shards))
        return jnp.repeat(jnp.exp(heights), extent[axis_at] // blocks).reshape((-1,) + (1,) * (len(extent) - axis_at - 1))

    loudness = one(*shards[0])
    for cut in shards[1:]:
        loudness = loudness * one(*cut)
    return loudness


def noise(stream_key, shape, spread, reach, shards=(), kind=jnp.bfloat16):
    drawn = spread * jax.random.normal(stream_key, shape, jnp.float32)
    if shards:
        drawn = drawn * levels(stream_key, shape, shards, -0.22, 0.18)
    return jnp.clip(drawn, -reach, reach).astype(kind)


def setup_inputs(seed: int = 0) -> dict:
    seeds = jax.random.split(jax.random.key(seed), 6)
    acts = noise(seeds[0], (LAYERS, ROWS, D), 1.0, 6.0, ((0, 16), (1, 32)))
    grads = noise(seeds[1], (LAYERS, ROWS, D), 1.0, 6.0, ((0, 16), (1, 32)))
    in_factor = noise(seeds[2], (LAYERS, D, KIN), D ** -0.5, 0.078125, ((0, 16),))
    out_factor = noise(seeds[3], (LAYERS, D, KOUT), D ** -0.5, 0.078125, ((0, 16),))
    clip_tokens = draw_clip_tokens(jax.random.fold_in(seeds[5], 71), 0)
    return {"acts": acts, "grads": grads, "in_factor": in_factor, "out_factor": out_factor, "clip_tokens": clip_tokens}


def block_sketch(u_rows, v_rows, counts):
    row_count = u_rows.shape[1]
    starts = jnp.cumsum(counts, axis=-1) - counts
    position = jnp.arange(row_count, dtype=jnp.int32)
    member = ((position[None, None, :] >= starts[..., None]) & (position[None, None, :] < (starts + counts)[..., None])).astype(jnp.bfloat16)
    masked = member[..., None] * u_rows[:, None, :, :]
    summed = jnp.einsum('bcro,bri->bcoi', masked, v_rows, preferred_element_type=jnp.float32)
    summed = summed * (1.0 / jnp.sqrt(counts.astype(jnp.float32)))[..., None, None]
    return summed.reshape(counts.shape[0] * counts.shape[1], -1).astype(jnp.bfloat16)

def reference(acts, grads, in_factor, out_factor, clip_tokens):
    counts = clip_tokens.reshape(N_CLIP, CLIPS_DEV)
    total = jnp.zeros((CLIPS, CLIPS), jnp.float32)
    for layer_index in range(LAYERS):
        v_rows = jnp.dot(acts[layer_index], in_factor[layer_index], preferred_element_type=jnp.float32).astype(jnp.bfloat16)
        u_rows = jnp.dot(grads[layer_index], out_factor[layer_index], preferred_element_type=jnp.float32).astype(jnp.bfloat16)
        sketch = block_sketch(u_rows.reshape(N_CLIP, CAP, KOUT), v_rows.reshape(N_CLIP, CAP, KIN), counts)
        total = total + jnp.dot(sketch, sketch.T, preferred_element_type=jnp.float32)
    return total * (1.0 / math.sqrt(LAYERS * KIN * KOUT))
```

```python
import functools
import math

import jax
import jax.numpy as jnp
from jax import lax
from jax.experimental import pallas as pl
from jax.experimental.pallas import tpu as pltpu
from jax.sharding import PartitionSpec as P

MESH = pl.DeviceIdType.MESH
NT = (((1,), (1,)), ((), ()))
ROWS = 256
CLIPS = 32
WIDE = 64
IDS = 16
PIECES = 4


def dot_nt(a, b):
    return lax.dot_general(a, b, NT, preferred_element_type=jnp.float32)


def inverse_root(n):
    r = lax.rsqrt(n)
    return r * (1.5 - 0.5 * n * r * r)


def kernel(
    acts, grads, in_t, out_t, tokens, out,
    abuf, gbuf, ibuf, obuf, blocks, pool_r, pool_c, scale_r, scale_c,
    part, near, half, far,
    load_sem, send1, recv1, send2, recv2, send3, recv3,
):
    clip, layer = lax.axis_index("clip"), lax.axis_index("layer")
    z, x, core = clip // 8, (clip // 2) % 4, clip % 2
    y, zh = layer // 4, layer % 4

    def at(clip_bits, layer_bits):
        return (jnp.bitwise_xor(clip, clip_bits), jnp.bitwise_xor(layer, layer_bits))

    loads = [
        pltpu.make_async_copy(in_t.at[0], ibuf, load_sem.at[0]),
        pltpu.make_async_copy(out_t.at[0], obuf, load_sem.at[1]),
    ]
    step = ROWS // PIECES
    for i in range(PIECES):
        rows = pl.ds(i * step, step)
        loads.append(pltpu.make_async_copy(acts.at[0, rows], abuf.at[rows], load_sem.at[2 + 2 * i]))
        loads.append(pltpu.make_async_copy(grads.at[0, rows], gbuf.at[rows], load_sem.at[3 + 2 * i]))
    for load in loads:
        load.start()

    peers = [(1, 0)]
    peers += [(8 * d, 0) for d in range(1, 4)]
    peers += [(2 * dx, 4 * dy) for dx in range(4) for dy in range(4) if dx or dy]
    peers += [(0, d) for d in range(1, 4)]
    barrier = pltpu.get_barrier_semaphore()
    for bits in peers:
        pl.semaphore_signal(barrier, inc=1, device_id=at(*bits), device_id_type=MESH)

    place = lax.broadcasted_iota(jnp.int32, (IDS, 128), 0) * 128 + lax.broadcasted_iota(
        jnp.int32, (IDS, 128), 1
    )
    owner = jnp.zeros((IDS, 128), jnp.int32)
    end = jnp.int32(0)
    for c in range(CLIPS - 1):
        end = end + tokens[c]
        owner = owner + jnp.where(place >= end, 1, 0)
    blocks[0, ROWS:, :] = owner.astype(jnp.float32).astype(jnp.bfloat16)

    loads[0].wait()
    loads[1].wait()
    for i in range(PIECES):
        rows = pl.ds(i * step, step)
        loads[2 + 2 * i].wait()
        loads[3 + 2 * i].wait()
        v = dot_nt(abuf[rows, :], ibuf[...])
        u = dot_nt(gbuf[rows, :], obuf[...])
        blocks[0, rows, :] = jnp.concatenate([u, v], axis=1).astype(jnp.bfloat16)

    pl.semaphore_wait(barrier, len(peers))

    def send_block(src, dst, bits):
        copy = pltpu.make_async_remote_copy(
            src_ref=blocks.at[src], dst_ref=blocks.at[dst], send_sem=send1.at[dst],
            recv_sem=recv1.at[dst], device_id=at(bits, 0), device_id_type=MESH,
        )
        copy.start()
        return copy

    copies = {}
    for d in (3, 2, 1):
        copies[4 + d] = send_block(0, 4 + d, 8 * d)
    copies[4] = send_block(0, 4, 1)
    for d in (2, 1, 3):
        copies[d] = send_block(0, d, 2 * d)

    lane = lax.broadcasted_iota(jnp.int32, (1, 128), 1)

    def row_pool(slot):
        ids = blocks[slot, ROWS:, :].astype(jnp.float32)
        which = lax.broadcasted_iota(jnp.int32, (CLIPS, 128), 0).astype(jnp.float32)
        hot = jnp.concatenate(
            [jnp.where(which == ids[i : i + 1, :], 1.0, 0.0) for i in range(2)], axis=1
        )
        pool_r[slot] = hot.astype(jnp.bfloat16)
        scale = inverse_root(jnp.sum(hot, axis=1, keepdims=True))
        scale_r[slot] = jnp.where(lane < 64, scale[0:16], scale[16:32])

    def col_pool(slot, side):
        ids = blocks[slot, ROWS:, :].astype(jnp.float32)
        j = lax.broadcasted_iota(jnp.int32, (128, 128), 0)
        which = jnp.where((j // CLIPS) % 2 == side, j % CLIPS, -1).astype(jnp.float32)
        hot = jnp.concatenate(
            [jnp.where(which == ids[i : i + 1, :], 1.0, 0.0) for i in range(2)], axis=1
        ).astype(jnp.bfloat16)
        return hot

    def unit(dx, dz, same, other):
        rows = blocks[dx, pl.ds(0, ROWS), :]
        row_u = jnp.where(lane < WIDE, rows, jnp.zeros_like(rows))
        row_v = jnp.where(lane < WIDE, jnp.zeros_like(rows), rows)
        pooled = jnp.zeros((ROWS, 128), jnp.float32)
        for k, slot in enumerate((same, other)):
            cols = blocks[slot, 0:ROWS, :]
            gram = (dot_nt(row_u, cols) * dot_nt(row_v, cols)).astype(jnp.bfloat16)
            pooled = pooled + dot_nt(gram, pool_c[dz, k])
        tile = jnp.dot(pool_r[dx], pooled.astype(jnp.bfloat16), preferred_element_type=jnp.float32)
        packed = jnp.where(lane < 64, tile[0:16], tile[16:32])
        return packed * scale_r[dx] * scale_c[dz, 0:1, :]

    def to_near(dx, dz):
        dy = jnp.bitwise_xor(jnp.bitwise_xor(y, z), dz)
        slot = dx * 4 + dy
        copy = pltpu.make_async_remote_copy(
            src_ref=part.at[dz, dx], dst_ref=near.at[slot], send_sem=send2.at[dz * 4 + dx],
            recv_sem=recv2.at[slot], device_id=at(2 * dx, 4 * dy), device_id_type=MESH,
        )
        return slot, copy

    for dz in range(4):
        same, other = (0, 4) if dz == 0 else (4 + dz, 7 + dz)
        if dz:
            copies[same].wait_recv()
            copies[other] = send_block(same, other, 1)
        copies[other].wait_recv()
        for k, slot in enumerate((same, other)):
            pool_c[dz, k] = col_pool(slot, core if k == 0 else 1 - core)
        counts = sum(dot_nt(jnp.ones((16, ROWS), jnp.bfloat16), pool_c[dz, k]) for k in range(2))
        scale_c[dz] = inverse_root(counts)
        if dz == 0:
            row_pool(0)

        for dx in range(4):
            if dz == 0 and dx:
                copies[dx].wait_recv()
                row_pool(dx)
            part[dz, dx] = unit(dx, dz, same, other)
            slot, copy = to_near(dx, dz)
            if dx:
                copy.start()
            else:

                @pl.when(slot != 0)
                def _():
                    copy.start()

                @pl.when(slot == 0)
                def _():
                    near[0] = part[dz, 0]

    def gathered(d):
        dx = jnp.bitwise_xor(jnp.bitwise_xor(x, zh), d)
        total = jnp.zeros((16, 128), jnp.float32)
        for dy in range(4):
            slot = dx * 4 + dy
            arrival = pltpu.make_async_remote_copy(
                src_ref=part.at[0, 0], dst_ref=near.at[slot], send_sem=send2.at[0],
                recv_sem=recv2.at[slot], device_id=at(1, 0), device_id_type=MESH,
            )
            if dy:
                arrival.wait_recv()
            else:

                @pl.when(slot != 0)
                def _():
                    arrival.wait_recv()

            total = total + near[slot]
        return total

    last = []
    for d in (2, 1, 3):
        half[d] = gathered(d)
        copy = pltpu.make_async_remote_copy(
            src_ref=half.at[d], dst_ref=far.at[d], send_sem=send3.at[d], recv_sem=recv3.at[d],
            device_id=at(0, d), device_id_type=MESH,
        )
        copy.start()
        last.append(copy)
    total = gathered(0)
    for copy, d in zip(last, (2, 1, 3), strict=True):
        copy.wait_recv()
        total = total + far[d]
    total = total * (1.0 / math.sqrt(16 * WIDE * WIDE))
    out[0:16, :] = total[:, 0:64]
    out[16:32, :] = total[:, 64:128]

    for copy in copies.values():
        copy.wait_send()
    for dz in range(4):
        for dx in range(4):
            slot, copy = to_near(dx, dz)
            if dx:
                copy.wait_send()
            else:

                @pl.when(slot != 0)
                def _():
                    copy.wait_send()

    for copy in last:
        copy.wait_send()


def body(acts, grads, in_factor, out_factor, clip_tokens):
    depth = acts.shape[2]
    bf16, f32 = jnp.bfloat16, jnp.float32
    hbm = pl.BlockSpec(memory_space=pltpu.HBM)
    return pl.pallas_call(
        kernel,
        out_shape=jax.ShapeDtypeStruct((CLIPS, 64), f32),
        in_specs=[hbm] * 4 + [pl.BlockSpec(memory_space=pltpu.SMEM)],
        out_specs=pl.BlockSpec(memory_space=pltpu.VMEM),
        scratch_shapes=[
            pltpu.VMEM((ROWS, depth), bf16),
            pltpu.VMEM((ROWS, depth), bf16),
            pltpu.VMEM((WIDE, depth), bf16),
            pltpu.VMEM((WIDE, depth), bf16),
            pltpu.VMEM((11, ROWS + IDS, 128), bf16),
            pltpu.VMEM((4, CLIPS, ROWS), bf16),
            pltpu.VMEM((4, 2, 128, ROWS), bf16),
            pltpu.VMEM((4, 16, 128), f32),
            pltpu.VMEM((4, 16, 128), f32),
            pltpu.VMEM((4, 4, 16, 128), f32),
            pltpu.VMEM((16, 16, 128), f32),
            pltpu.VMEM((4, 16, 128), f32),
            pltpu.VMEM((4, 16, 128), f32),
            pltpu.SemaphoreType.DMA((2 + 2 * PIECES,)),
            pltpu.SemaphoreType.DMA((11,)),
            pltpu.SemaphoreType.DMA((11,)),
            pltpu.SemaphoreType.DMA((16,)),
            pltpu.SemaphoreType.DMA((16,)),
            pltpu.SemaphoreType.DMA((4,)),
            pltpu.SemaphoreType.DMA((4,)),
        ],
        compiler_params=pltpu.CompilerParams(
            collective_id=0, has_side_effects=True, vmem_limit_bytes=60 * 1024 * 1024
        ),
        cost_estimate=pl.CostEstimate(flops=10**9, bytes_accessed=7 * 10**6, transcendentals=0),
        name="similarity",
    )(
        acts,
        grads,
        jnp.swapaxes(in_factor, 1, 2),
        jnp.swapaxes(out_factor, 1, 2),
        clip_tokens,
    )


def solution(mesh):
    return jax.shard_map(
        body,
        mesh=mesh,
        in_specs=(
            P("layer", "clip", None),
            P("layer", "clip", None),
            P("layer", None, None),
            P("layer", None, None),
            P("clip"),
        ),
        out_specs=P("clip", "layer"),
        check_vma=False,
    )
```

```python
import functools
import math

import jax
import jax.numpy as jnp
from jax import lax
from jax.experimental import pallas as pl
from jax.experimental.pallas import tpu as pltpu
from jax.sharding import PartitionSpec as P

MESH = pl.DeviceIdType.MESH
NT = (((1,), (1,)), ((), ()))
ROWS = 256
CLIPS = 32
WIDE = 64
IDS = 16
PIECES = 4


def dot_nt(a, b):
    return lax.dot_general(a, b, NT, preferred_element_type=jnp.float32)


def inverse_root(n):
    r = lax.rsqrt(n)
    return r * (1.5 - 0.5 * n * r * r)


def kernel(
    acts, grads, in_t, out_t, tokens, out,
    abuf, gbuf, ibuf, obuf, blocks, pairs, pool_r, pool_c, scale_r, scale_c,
    held, part, near, half, far,
    load_sem, send1, recv1, send2, recv2, send3, recv3,
    counts, counts_sem, plane_in, other_in, edge_in, next_in, edge_two, two_in,
):
    clip, layer = lax.axis_index("clip"), lax.axis_index("layer")
    z, x, core = clip // 8, (clip // 2) % 4, clip % 2
    y, zh = layer // 4, layer % 4

    def at(clip_bits, layer_bits):
        return (jnp.bitwise_xor(clip, clip_bits), jnp.bitwise_xor(layer, layer_bits))

    token_load = pltpu.make_async_copy(tokens, counts, counts_sem)
    token_load.start()
    loads = [
        pltpu.make_async_copy(in_t.at[0], ibuf, load_sem.at[0]),
        pltpu.make_async_copy(out_t.at[0], obuf, load_sem.at[1]),
    ]
    step = ROWS // PIECES
    for i in range(PIECES):
        rows = pl.ds(i * step, step)
        loads.append(pltpu.make_async_copy(acts.at[0, rows], abuf.at[rows], load_sem.at[2 + 2 * i]))
        loads.append(pltpu.make_async_copy(grads.at[0, rows], gbuf.at[rows], load_sem.at[3 + 2 * i]))
    for load in loads:
        load.start()

    peers = [(8 * d, 0) for d in range(1, 4)]
    peers += [(d, 0) for d in (1, 2, 4, 6)]
    peers += [(0, 4 * d) for d in range(1, 4)]
    low, high = z == 0, z == 3
    edge = jnp.logical_or(low, high)
    on_edge = jnp.where(edge, 1, 0)
    across = (jnp.bitwise_xor(clip, 24), y * 4 + lax.rem(zh + jnp.where(high, 1, 3), 4))
    barrier = pltpu.get_barrier_semaphore()

    def tell(sem, device):
        pl.semaphore_signal(sem, inc=1, device_id=device, device_id_type=MESH)

    for bits in peers:
        tell(barrier, at(*bits))

    @pl.when(edge)
    def _():
        tell(barrier, across)

    place = lax.broadcasted_iota(jnp.int32, (IDS, 128), 0) * 128 + lax.broadcasted_iota(
        jnp.int32, (IDS, 128), 1
    )
    owner = jnp.zeros((IDS, 128), jnp.int32)
    end = jnp.int32(0)
    token_load.wait()
    for c in range(CLIPS - 1):
        end = end + counts[c]
        owner = owner + jnp.where(place >= end, 1, 0)
    blocks[0, ROWS:, :] = owner.astype(jnp.float32).astype(jnp.bfloat16)

    loads[0].wait()
    loads[1].wait()
    for i in range(PIECES):
        rows = pl.ds(i * step, step)
        loads[2 + 2 * i].wait()
        loads[3 + 2 * i].wait()
        v = dot_nt(abuf[rows, :], ibuf[...])
        u = dot_nt(gbuf[rows, :], obuf[...])
        blocks[0, rows, :] = jnp.concatenate([u, v], axis=1).astype(jnp.bfloat16)

    pl.semaphore_wait(barrier, len(peers) + on_edge)

    def send_block(src, slot, bits):
        copy = pltpu.make_async_remote_copy(
            src_ref=blocks.at[src], dst_ref=blocks.at[slot], send_sem=send1.at[slot],
            recv_sem=recv1.at[slot], device_id=at(bits, 0), device_id_type=MESH,
        )
        copy.start()
        return copy

    sends = [send_block(0, 1, 1)]
    for d in (1, 3, 2):
        sends.append(send_block(0, 2 * d, 2 * d))
        sends.append(send_block(0, 7 + d, 8 * d))

    for d in (2, 4, 6):
        tell(plane_in, at(d, 0))

    @pl.when(edge)
    def _():
        tell(edge_in, across)

    def relay_one():
        @pl.when(edge)
        def _():
            pl.semaphore_wait(edge_in, 1)
            for d in range(1, 4):
                tell(next_in, at(8 * d, 0))

    def relay_two():
        pl.semaphore_wait(next_in, 2 - on_edge)

        @pl.when(high)
        def _():
            tell(edge_two, across)

    def relay_three():
        @pl.when(low)
        def _():
            pl.semaphore_wait(edge_two, 1)
            for d in range(1, 4):
                tell(two_in, at(8 * d, 0))

    def relay_four():
        @pl.when(jnp.logical_not(low))
        def _():
            pl.semaphore_wait(two_in, 1)

    def block_arrives(slot):
        pltpu.make_async_remote_copy(
            src_ref=blocks.at[0], dst_ref=blocks.at[slot], send_sem=send1.at[slot],
            recv_sem=recv1.at[slot], device_id=at(1, 0), device_id_type=MESH,
        ).wait_recv()

    lane = lax.broadcasted_iota(jnp.int32, (1, 128), 1)
    group = lane // CLIPS

    def by_group(pieces):
        out = pieces[0]
        for g in range(1, 4):
            out = jnp.where(group == g, pieces[g], out)
        return out

    def hot_ids(slot, which):
        ids = blocks[slot, ROWS:, :].astype(jnp.float32)
        halves = [jnp.where(which == ids[i : i + 1, :], 1.0, 0.0) for i in range(2)]
        return jnp.concatenate(halves, axis=1)

    def place_of(own, k):
        return own if k == 0 else (4 - k) - jnp.where(own >= 4 - k, 1, 0)

    def bits_of(own, k):
        return 0 if k == 0 else jnp.bitwise_xor(own, place_of(own, k))

    def row_slot(kx, i):
        return 2 * bits_of(x, kx) + i

    def take_rows(kx):
        for i in range(2):
            slot = row_slot(kx, i)
            if i:
                block_arrives(slot)
            hot = hot_ids(slot, lax.broadcasted_iota(jnp.int32, (CLIPS, 128), 0).astype(jnp.float32))
            pool_r[kx, i] = hot.astype(jnp.bfloat16)
            scale = inverse_root(jnp.sum(hot, axis=1, keepdims=True))
            scale_r[kx, i] = by_group([scale[8 * g : 8 * g + 8] for g in range(4)])

    def take_cols(kz):
        slot = 0
        if kz:
            slot = 7 + bits_of(z, kz)
            block_arrives(slot)
        cols = blocks[slot, pl.ds(0, ROWS), :]
        pairs[kz, 0:ROWS] = jnp.where(lane < WIDE, cols, jnp.zeros_like(cols))
        pairs[kz, ROWS:] = jnp.where(lane < WIDE, jnp.zeros_like(cols), cols)
        j = lax.broadcasted_iota(jnp.int32, (128, 128), 0)
        which = jnp.where((j // CLIPS) % 2 == kz % 2, j % CLIPS, -1).astype(jnp.float32)
        hot = hot_ids(slot, which).astype(jnp.bfloat16)
        pool_c[kz] = hot
        count = dot_nt(jnp.ones((16, ROWS), jnp.bfloat16), hot)[0:8]
        scale_c[kz] = inverse_root(count + pltpu.roll(count, CLIPS, 1))

    def to_near(kx, i, kz):
        bits, dy = row_slot(kx, i), jnp.bitwise_xor(y, place_of(z, kz))
        slot = bits * 4 + dy
        copy = pltpu.make_async_remote_copy(
            src_ref=part.at[kz, kx, i], dst_ref=near.at[slot], send_sem=send2.at[kz * 8 + kx * 2 + i],
            recv_sem=recv2.at[slot], device_id=at(bits, 4 * dy), device_id_type=MESH,
        )
        return slot, copy

    def pooled_pairs(kx, kz):
        rows = [blocks[row_slot(kx, i), pl.ds(0, ROWS), :] for i in range(2)]
        gram = dot_nt(jnp.concatenate(rows, axis=0), pairs[kz])
        gram = (gram[:, 0:ROWS] * gram[:, ROWS:]).astype(jnp.bfloat16)
        return dot_nt(gram, pool_c[kz])

    def finish(kx, kz, pooled):
        for i in range(2):
            tile = jnp.dot(
                pool_r[kx, i],
                pooled[i * ROWS : (i + 1) * ROWS].astype(jnp.bfloat16),
                preferred_element_type=jnp.float32,
            )
            moved = pltpu.roll(tile, CLIPS, 1)
            for n, k in enumerate((kz - 1, kz)):
                pieces = [(moved if (g + n) % 2 else tile)[8 * g : 8 * g + 8] for g in range(4)]
                part[k, kx, i] = by_group(pieces) * scale_r[kx, i] * scale_c[k]
                slot, copy = to_near(kx, i, k)
                if kx or i:
                    copy.start()
                else:

                    @pl.when(slot != 0)
                    def _():
                        copy.start()

                    @pl.when(slot == 0)
                    def _():
                        near[0] = part[k, 0, 0]

    take_cols(0)
    take_rows(0)
    held[0] = pooled_pairs(0, 0)
    relay_one()
    for kx in (1, 2, 3):
        slot = row_slot(kx, 0)
        block_arrives(slot)
        sends.append(send_block(slot, slot + 1, 1))
    for kx in (1, 2, 3):
        take_rows(kx)
        held[kx] = pooled_pairs(kx, 0)
    relay_two()
    take_cols(1)
    pl.semaphore_wait(plane_in, 3)
    tell(other_in, at(1, 0))
    pl.semaphore_wait(other_in, 1)
    for kx in range(4):
        finish(kx, 1, held[kx] + pooled_pairs(kx, 1))
    relay_three()
    take_cols(2)
    for kx in range(4):
        held[kx] = pooled_pairs(kx, 2)
    take_cols(3)
    for kx in range(4):
        finish(kx, 3, held[kx] + pooled_pairs(kx, 3))
    relay_four()

    def gathered(d, dc):
        bits = 2 * jnp.bitwise_xor(jnp.bitwise_xor(x, zh), d) + dc
        total = jnp.zeros((8, 128), jnp.float32)
        for dy in range(4):
            slot = bits * 4 + dy
            arrival = pltpu.make_async_remote_copy(
                src_ref=part.at[0, 0, 0], dst_ref=near.at[slot], send_sem=send2.at[0],
                recv_sem=recv2.at[slot], device_id=at(1, 0), device_id_type=MESH,
            )
            if dc or dy:
                arrival.wait_recv()
            else:

                @pl.when(slot != 0)
                def _():
                    arrival.wait_recv()

            total = total + near[slot]
        return total

    last = []
    for d in (2, 1, 3):
        for dc in range(2):
            half[d, dc] = gathered(d, dc)
        copy = pltpu.make_async_remote_copy(
            src_ref=half.at[d], dst_ref=far.at[d], send_sem=send3.at[d], recv_sem=recv3.at[d],
            device_id=at(0, d), device_id_type=MESH,
        )
        copy.start()
        last.append(copy)
    total = [gathered(0, dc) for dc in range(2)]
    for copy, d in zip(last, (2, 1, 3), strict=True):
        copy.wait_recv()
        total = [total[dc] + far[d, dc] for dc in range(2)]
    norm = 1.0 / math.sqrt(16 * WIDE * WIDE)
    for side in range(2):
        mine = jnp.where(core == side, total[0], total[1]) * norm
        for g in range(4):
            out[8 * g : 8 * g + 8, CLIPS * side : CLIPS * (side + 1)] = mine[:, CLIPS * g : CLIPS * (g + 1)]

    for copy in sends:
        copy.wait_send()
    for kz in range(4):
        for kx in range(4):
            for i in range(2):
                slot, copy = to_near(kx, i, kz)
                if kx or i:
                    copy.wait_send()
                else:

                    @pl.when(slot != 0)
                    def _():
                        copy.wait_send()

    for copy in last:
        copy.wait_send()


def body(acts, grads, in_factor, out_factor, clip_tokens):
    depth = acts.shape[2]
    bf16, f32 = jnp.bfloat16, jnp.float32
    hbm = pl.BlockSpec(memory_space=pltpu.HBM)
    return pl.pallas_call(
        kernel,
        out_shape=pltpu.VMEM((CLIPS, 64), f32),
        in_specs=[hbm] * 4 + [hbm],
        out_specs=pl.BlockSpec(memory_space=pltpu.VMEM),
        scratch_shapes=[
            pltpu.VMEM((ROWS, depth), bf16),
            pltpu.VMEM((ROWS, depth), bf16),
            pltpu.VMEM((WIDE, depth), bf16),
            pltpu.VMEM((WIDE, depth), bf16),
            pltpu.VMEM((11, ROWS + IDS, 128), bf16),
            pltpu.VMEM((4, 2 * ROWS, 128), bf16),
            pltpu.VMEM((4, 2, CLIPS, ROWS), bf16),
            pltpu.VMEM((4, 128, ROWS), bf16),
            pltpu.VMEM((4, 2, 8, 128), f32),
            pltpu.VMEM((4, 8, 128), f32),
            pltpu.VMEM((4, 2 * ROWS, 128), f32),
            pltpu.VMEM((4, 4, 2, 8, 128), f32),
            pltpu.VMEM((32, 8, 128), f32),
            pltpu.VMEM((4, 2, 8, 128), f32),
            pltpu.VMEM((4, 2, 8, 128), f32),
            pltpu.SemaphoreType.DMA((2 + 2 * PIECES,)),
            pltpu.SemaphoreType.DMA((11,)),
            pltpu.SemaphoreType.DMA((11,)),
            pltpu.SemaphoreType.DMA((32,)),
            pltpu.SemaphoreType.DMA((32,)),
            pltpu.SemaphoreType.DMA((4,)),
            pltpu.SemaphoreType.DMA((4,)),
        ]
        + [pltpu.SMEM((CLIPS,), jnp.int32), pltpu.SemaphoreType.DMA(())]
        + [pltpu.SemaphoreType.REGULAR] * 6,
        compiler_params=pltpu.CompilerParams(
            collective_id=0, has_side_effects=True, vmem_limit_bytes=60 * 1024 * 1024
        ),
        cost_estimate=pl.CostEstimate(flops=10**9, bytes_accessed=7 * 10**6, transcendentals=0),
        name="similarity",
    )(
        acts,
        grads,
        jnp.swapaxes(in_factor, 1, 2),
        jnp.swapaxes(out_factor, 1, 2),
        clip_tokens,
    )


def solution(mesh):
    return jax.shard_map(
        body,
        mesh=mesh,
        in_specs=(
            P("layer", "clip", None),
            P("layer", "clip", None),
            P("layer", None, None),
            P("layer", None, None),
            P("clip"),
        ),
        out_specs=P("clip", "layer"),
        check_vma=False,
    )
```

```python
import functools
import math

import jax
import jax.numpy as jnp
from jax import lax
from jax.experimental import pallas as pl
from jax.experimental.pallas import tpu as pltpu
from jax.sharding import PartitionSpec as P

MESH = pl.DeviceIdType.MESH
NT = (((1,), (1,)), ((), ()))
ROWS = 256
CLIPS = 32
WIDE = 64
IDS = 16
PIECES = 4


def dot_nt(a, b):
    return lax.dot_general(a, b, NT, preferred_element_type=jnp.float32)


def inverse_root(n):
    r = lax.rsqrt(n)
    return r * (1.5 - 0.5 * n * r * r)


def kernel(
    acts, grads, in_t, out_t, tokens, out,
    abuf, gbuf, ibuf, obuf, blocks, pairs, pool_r, pool_c, scale_r, scale_c,
    held, part, near, half, far,
    load_sem, send1, recv1, send2, recv2, send3, recv3, recv4,
    counts, counts_sem, plane_in, other_in, run_in, edge_in, next_in, edge_two, two_in,
):
    clip, layer = lax.axis_index("clip"), lax.axis_index("layer")
    z, x, core = clip // 8, (clip // 2) % 4, clip % 2
    y, zh = layer // 4, layer % 4

    turn = jnp.where(zh >= 2, z, 3 - z)

    def by_turn(values):
        return sum(jnp.where(turn == n, value, 0) for n, value in enumerate(values))

    takes = (by_turn((3, 3, 2, 1)), by_turn((0, 1, 0, 2)))
    gives = (by_turn((1, 2, 3, 3)), by_turn((2, 0, 1, 0)))
    takes_two, gives_two = turn % 2 == 1, turn % 2 == 0
    apart = jnp.bitwise_xor(y, z)
    mine = (apart == 0) | (apart == takes[0]) | (takes_two & (apart == takes[1]))

    def at(clip_bits, layer_bits):
        return (jnp.bitwise_xor(clip, clip_bits), jnp.bitwise_xor(layer, layer_bits))

    token_load = pltpu.make_async_copy(tokens, counts, counts_sem)
    token_load.start()
    loads = [
        pltpu.make_async_copy(in_t.at[0], ibuf, load_sem.at[0]),
        pltpu.make_async_copy(out_t.at[0], obuf, load_sem.at[1]),
    ]
    step = ROWS // PIECES
    for i in range(PIECES):
        rows = pl.ds(i * step, step)
        loads.append(pltpu.make_async_copy(acts.at[0, rows], abuf.at[rows], load_sem.at[2 + 2 * i]))
        loads.append(pltpu.make_async_copy(grads.at[0, rows], gbuf.at[rows], load_sem.at[3 + 2 * i]))
    for load in loads:
        load.start()

    peers = [(8 * d, 0) for d in range(1, 4)]
    peers += [(d, 0) for d in (1, 2, 4, 6)]
    peers += [(0, 4 * d) for d in range(1, 4)]
    low, high = z == 0, z == 3
    edge = jnp.logical_or(low, high)
    on_edge = jnp.where(edge, 1, 0)
    across = (jnp.bitwise_xor(clip, 24), y * 4 + lax.rem(zh + jnp.where(high, 1, 3), 4))
    barrier = pltpu.get_barrier_semaphore()

    def tell(sem, device):
        pl.semaphore_signal(sem, inc=1, device_id=device, device_id_type=MESH)

    for bits in peers:
        tell(barrier, at(*bits))

    @pl.when(edge)
    def _():
        tell(barrier, across)

    place = lax.broadcasted_iota(jnp.int32, (IDS, 128), 0) * 128 + lax.broadcasted_iota(
        jnp.int32, (IDS, 128), 1
    )
    owner = jnp.zeros((IDS, 128), jnp.int32)
    end = jnp.int32(0)
    token_load.wait()
    for c in range(CLIPS - 1):
        end = end + counts[c]
        owner = owner + jnp.where(place >= end, 1, 0)
    blocks[0, ROWS:, :] = owner.astype(jnp.float32).astype(jnp.bfloat16)

    loads[0].wait()
    loads[1].wait()
    for i in range(PIECES):
        rows = pl.ds(i * step, step)
        loads[2 + 2 * i].wait()
        loads[3 + 2 * i].wait()
        v = dot_nt(abuf[rows, :], ibuf[...])
        u = dot_nt(gbuf[rows, :], obuf[...])
        blocks[0, rows, :] = jnp.concatenate([u, v], axis=1).astype(jnp.bfloat16)

    pl.semaphore_wait(barrier, len(peers) + on_edge)

    def send_block(src, slot, bits):
        copy = pltpu.make_async_remote_copy(
            src_ref=blocks.at[src], dst_ref=blocks.at[slot], send_sem=send1.at[slot],
            recv_sem=recv1.at[slot], device_id=at(bits, 0), device_id_type=MESH,
        )
        copy.start()
        return copy

    def column_send(n):
        return pltpu.make_async_remote_copy(
            src_ref=blocks.at[0], dst_ref=blocks.at[7 + gives[n]], send_sem=send1.at[8 + n],
            recv_sem=recv1.at[7 + gives[n]], device_id=at(8 * gives[n], 0), device_id_type=MESH,
        )

    sends = [send_block(0, 1, 1), send_block(0, 2, 2)]
    column_send(0).start()
    sends.append(send_block(0, 6, 6))

    @pl.when(gives_two)
    def _():
        column_send(1).start()

    sends.append(send_block(0, 4, 4))

    for d in range(1, 4):
        tell(plane_in, at(2 * d, 0))
        tell(run_in, at(8 * d, 0))

    @pl.when(edge)
    def _():
        tell(edge_in, across)

    def relay_one():
        @pl.when(edge)
        def _():
            pl.semaphore_wait(edge_in, 1)
            for d in range(1, 4):
                tell(next_in, at(8 * d, 0))

    def relay_two():
        pl.semaphore_wait(next_in, 2 - on_edge)

        @pl.when(high)
        def _():
            tell(edge_two, across)

    def relay_three():
        @pl.when(low)
        def _():
            pl.semaphore_wait(edge_two, 1)
            for d in range(1, 4):
                tell(two_in, at(8 * d, 0))

    def relay_four():
        @pl.when(jnp.logical_not(low))
        def _():
            pl.semaphore_wait(two_in, 1)

    def block_arrives(slot):
        pltpu.make_async_remote_copy(
            src_ref=blocks.at[0], dst_ref=blocks.at[slot], send_sem=send1.at[slot],
            recv_sem=recv1.at[slot], device_id=at(1, 0), device_id_type=MESH,
        ).wait_recv()

    lane = lax.broadcasted_iota(jnp.int32, (1, 128), 1)
    group = lane // CLIPS

    def by_group(pieces):
        out = pieces[0]
        for g in range(1, 4):
            out = jnp.where(group == g, pieces[g], out)
        return out

    def hot_ids(slot, which):
        ids = blocks[slot, ROWS:, :].astype(jnp.float32)
        halves = [jnp.where(which == ids[i : i + 1, :], 1.0, 0.0) for i in range(2)]
        return jnp.concatenate(halves, axis=1)

    def place_up(own, k):
        return own if k == 0 else (k - 1) + jnp.where(own <= k - 1, 1, 0)

    def bits_x(k):
        return 0 if k == 0 else jnp.bitwise_xor(x, place_up(x, k))

    def row_slot(kx, i):
        return 2 * bits_x(kx) + i

    def take_rows(kx):
        for i in range(2):
            slot = row_slot(kx, i)
            if i:
                block_arrives(slot)
            hot = hot_ids(slot, lax.broadcasted_iota(jnp.int32, (CLIPS, 128), 0).astype(jnp.float32))
            pool_r[kx, i] = hot.astype(jnp.bfloat16)
            scale = inverse_root(jnp.sum(hot, axis=1, keepdims=True))
            scale_r[kx, i] = by_group([scale[8 * g : 8 * g + 8] for g in range(4)])

    def take_cols(kz):
        slot = 0
        if kz:
            slot = 7 + takes[kz - 1]
            block_arrives(slot)
        cols = blocks[slot, pl.ds(0, ROWS), :]
        pairs[kz, 0:ROWS] = jnp.where(lane < WIDE, cols, jnp.zeros_like(cols))
        pairs[kz, ROWS:] = jnp.where(lane < WIDE, jnp.zeros_like(cols), cols)
        j = lax.broadcasted_iota(jnp.int32, (128, 128), 0)
        which = jnp.where((j // CLIPS) % 2 == kz % 2, j % CLIPS, -1).astype(jnp.float32)
        hot = hot_ids(slot, which).astype(jnp.bfloat16)
        pool_c[kz] = hot
        count = dot_nt(jnp.ones((16, ROWS), jnp.bfloat16), hot)[0:8]
        scale_c[kz] = inverse_root(count + pltpu.roll(count, CLIPS, 1))

    def to_near(kx, i, kz):
        bits = row_slot(kx, i)
        dy = jnp.bitwise_xor(apart, takes[kz - 1]) if kz else apart
        copy = pltpu.make_async_remote_copy(
            src_ref=part.at[kz, bits], dst_ref=near.at[dy, bits], send_sem=send2.at[kz * 8 + kx * 2 + i],
            recv_sem=recv2.at[dy * 8 + bits], device_id=at(bits, 4 * dy), device_id_type=MESH,
        )
        return dy * 8 + bits, copy

    def to_other_run(kz):
        return pltpu.make_async_remote_copy(
            src_ref=part.at[kz], dst_ref=near.at[apart], send_sem=send2.at[24 + kz],
            recv_sem=recv4.at[apart], device_id=at(8 * takes[kz - 1], 4 * apart), device_id_type=MESH,
        )

    def pooled_pairs(kx, kz):
        rows = [blocks[row_slot(kx, i), pl.ds(0, ROWS), :] for i in range(2)]
        gram = dot_nt(jnp.concatenate(rows, axis=0), pairs[kz])
        gram = (gram[:, 0:ROWS] * gram[:, ROWS:]).astype(jnp.bfloat16)
        return dot_nt(gram, pool_c[kz])

    def finish(kx, kzs, pooled):
        for i in range(2):
            tile = jnp.dot(
                pool_r[kx, i],
                pooled[i * ROWS : (i + 1) * ROWS].astype(jnp.bfloat16),
                preferred_element_type=jnp.float32,
            )
            moved = pltpu.roll(tile, CLIPS, 1)
            for n, k in enumerate(kzs):
                pieces = [(moved if (g + n) % 2 else tile)[8 * g : 8 * g + 8] for g in range(4)]
                part[k, row_slot(kx, i)] = by_group(pieces) * scale_r[kx, i] * scale_c[k]
                slot, copy = to_near(kx, i, k)
                if kx or i:
                    copy.start()
                else:

                    @pl.when(slot != 0)
                    def _():
                        copy.start()

                    @pl.when(slot == 0)
                    def _():
                        near[0, 0] = part[k, 0]

    take_cols(0)
    take_rows(0)
    held[0] = pooled_pairs(0, 0)
    relay_one()
    for kx in (1, 2, 3):
        slot = row_slot(kx, 0)
        block_arrives(slot)
        sends.append(send_block(slot, slot + 1, 1))
    for kx in (1, 2, 3):
        take_rows(kx)
        held[kx] = pooled_pairs(kx, 0)
    relay_two()
    pl.semaphore_wait(plane_in, 3)
    tell(other_in, at(1, 0))
    pl.semaphore_wait(run_in, 3)
    take_cols(1)
    pl.semaphore_wait(other_in, 1)
    for kx in range(4):
        finish(kx, (0, 1), held[kx] + pooled_pairs(kx, 1))
    to_other_run(1).start()
    relay_three()

    @pl.when(takes_two)
    def _():
        take_cols(2)
        for kx in range(4):
            finish(kx, (2,), pooled_pairs(kx, 2))
        to_other_run(2).start()

    relay_four()

    @pl.when(jnp.logical_not(mine))
    def _():
        for dy in range(4):
            pltpu.make_async_remote_copy(
                src_ref=part.at[0], dst_ref=near.at[dy], send_sem=send2.at[25],
                recv_sem=recv4.at[dy], device_id=at(1, 0), device_id_type=MESH,
            ).wait_recv()

    def gathered(d, dc):
        bits = 2 * jnp.bitwise_xor(jnp.bitwise_xor(x, zh), d) + dc
        total = jnp.zeros((8, 128), jnp.float32)
        for dy in range(4):
            slot = dy * 8 + bits
            arrival = pltpu.make_async_remote_copy(
                src_ref=part.at[0, 0], dst_ref=near.at[dy, bits], send_sem=send2.at[0],
                recv_sem=recv2.at[slot], device_id=at(1, 0), device_id_type=MESH,
            )

            @pl.when(mine & (slot != 0))
            def _():
                arrival.wait_recv()

            total = total + near[dy, bits]
        return total

    last = []
    for d in (2, 1, 3):
        for dc in range(2):
            half[d, dc] = gathered(d, dc)
        copy = pltpu.make_async_remote_copy(
            src_ref=half.at[d], dst_ref=far.at[d], send_sem=send3.at[d], recv_sem=recv3.at[d],
            device_id=at(0, d), device_id_type=MESH,
        )
        copy.start()
        last.append(copy)
    total = [gathered(0, dc) for dc in range(2)]
    for copy in last:
        copy.wait_recv()
    norm = 1.0 / math.sqrt(16 * WIDE * WIDE)
    for side in range(2):
        here, there = (
            jnp.where(core == side, pair[0], pair[1]) * norm
            for pair in ([total[dc] + far[1, dc] for dc in range(2)], [far[2, dc] + far[3, dc] for dc in range(2)])
        )
        straight = jnp.where(mine, here, there) + jnp.where(apart == 0, there, 0.0)
        crossed = jnp.where(apart == 0, 0.0, jnp.where(mine, there, here))
        straight, crossed = (
            jnp.concatenate([packed[:, CLIPS * g : CLIPS * (g + 1)] for g in range(4)], axis=0)
            for packed in (straight, crossed)
        )
        crossed = jnp.concatenate([crossed, jnp.zeros((CLIPS, 128 - CLIPS), jnp.float32)], axis=1)
        crossed = jnp.concatenate([crossed, jnp.zeros((128 - CLIPS, 128), jnp.float32)], axis=0)
        out[:, CLIPS * side : CLIPS * (side + 1)] = straight + crossed.T[0:CLIPS, 0:CLIPS]

    for copy in sends:
        copy.wait_send()
    column_send(0).wait_send()

    @pl.when(gives_two)
    def _():
        column_send(1).wait_send()

    def near_sent(kz):
        for kx in range(4):
            for i in range(2):
                slot, copy = to_near(kx, i, kz)
                if kx or i:
                    copy.wait_send()
                else:

                    @pl.when(slot != 0)
                    def _():
                        copy.wait_send()

        if kz:
            to_other_run(kz).wait_send()

    near_sent(0)
    near_sent(1)

    @pl.when(takes_two)
    def _():
        near_sent(2)

    for copy in last:
        copy.wait_send()


def body(acts, grads, in_factor, out_factor, clip_tokens):
    depth = acts.shape[2]
    bf16, f32 = jnp.bfloat16, jnp.float32
    hbm = pl.BlockSpec(memory_space=pltpu.HBM)
    return pl.pallas_call(
        kernel,
        out_shape=pltpu.VMEM((CLIPS, 64), f32),
        in_specs=[hbm] * 4 + [hbm],
        out_specs=pl.BlockSpec(memory_space=pltpu.VMEM),
        scratch_shapes=[
            pltpu.VMEM((ROWS, depth), bf16),
            pltpu.VMEM((ROWS, depth), bf16),
            pltpu.VMEM((WIDE, depth), bf16),
            pltpu.VMEM((WIDE, depth), bf16),
            pltpu.VMEM((11, ROWS + IDS, 128), bf16),
            pltpu.VMEM((4, 2 * ROWS, 128), bf16),
            pltpu.VMEM((4, 2, CLIPS, ROWS), bf16),
            pltpu.VMEM((4, 128, ROWS), bf16),
            pltpu.VMEM((4, 2, 8, 128), f32),
            pltpu.VMEM((4, 8, 128), f32),
            pltpu.VMEM((4, 2 * ROWS, 128), f32),
            pltpu.VMEM((3, 8, 8, 128), f32),
            pltpu.VMEM((4, 8, 8, 128), f32),
            pltpu.VMEM((4, 2, 8, 128), f32),
            pltpu.VMEM((4, 2, 8, 128), f32),
            pltpu.SemaphoreType.DMA((2 + 2 * PIECES,)),
            pltpu.SemaphoreType.DMA((11,)),
            pltpu.SemaphoreType.DMA((11,)),
            pltpu.SemaphoreType.DMA((32,)),
            pltpu.SemaphoreType.DMA((32,)),
            pltpu.SemaphoreType.DMA((4,)),
            pltpu.SemaphoreType.DMA((4,)),
            pltpu.SemaphoreType.DMA((4,)),
        ]
        + [pltpu.SMEM((CLIPS,), jnp.int32), pltpu.SemaphoreType.DMA(())]
        + [pltpu.SemaphoreType.REGULAR] * 7,
        compiler_params=pltpu.CompilerParams(
            collective_id=0, has_side_effects=True, vmem_limit_bytes=60 * 1024 * 1024
        ),
        cost_estimate=pl.CostEstimate(flops=10**9, bytes_accessed=7 * 10**6, transcendentals=0),
        name="similarity",
    )(
        acts,
        grads,
        jnp.swapaxes(in_factor, 1, 2),
        jnp.swapaxes(out_factor, 1, 2),
        clip_tokens,
    )


def solution(mesh):
    return jax.shard_map(
        body,
        mesh=mesh,
        in_specs=(
            P("layer", "clip", None),
            P("layer", "clip", None),
            P("layer", None, None),
            P("layer", None, None),
            P("clip"),
        ),
        out_specs=P("clip", "layer"),
        check_vma=False,
    )
```

```python
import functools
import math

import jax
import jax.numpy as jnp
from jax import lax
from jax.experimental import pallas as pl
from jax.experimental.pallas import tpu as pltpu
from jax.sharding import PartitionSpec as P

MESH = pl.DeviceIdType.MESH
NT = (((1,), (1,)), ((), ()))
ROWS = 256
CLIPS = 32
WIDE = 64
IDS = 16
PIECES = 4


def dot_nt(a, b):
    return lax.dot_general(a, b, NT, preferred_element_type=jnp.float32)


def inverse_root(n):
    r = lax.rsqrt(n)
    return r * (1.5 - 0.5 * n * r * r)


def kernel(
    acts, grads, in_t, out_t, tokens, out,
    abuf, gbuf, ibuf, obuf, blocks, pairs, pool_r, pool_c, scale_r, scale_c,
    held, part, near, half, far,
    load_sem, send1, recv1, send2, recv2, send3, recv3, recv4,
    counts, counts_sem, plane_in, other_in, run_in, edge_in, next_in, edge_two, two_in,
):
    clip, layer = lax.axis_index("clip"), lax.axis_index("layer")
    z, x, core = clip // 8, (clip // 2) % 4, clip % 2
    y, zh = layer // 4, layer % 4

    turn = jnp.where(zh >= 2, z, 3 - z)
    odd = turn % 2
    takes = (jnp.where(turn < 2, 3, 2), 1)
    gives = (jnp.where(turn < 2, 2, 3), 1)
    apart = jnp.bitwise_xor(y, z)

    def straight_from(dx):
        half = (dx // 2) == odd
        return (apart == 0) | (apart == takes[0]) | ((apart == 1) & half)

    def at(clip_bits, layer_bits):
        return (jnp.bitwise_xor(clip, clip_bits), jnp.bitwise_xor(layer, layer_bits))

    token_load = pltpu.make_async_copy(tokens, counts, counts_sem)
    token_load.start()
    loads = [
        pltpu.make_async_copy(in_t.at[0], ibuf, load_sem.at[0]),
        pltpu.make_async_copy(out_t.at[0], obuf, load_sem.at[1]),
    ]
    step = ROWS // PIECES
    for i in range(PIECES):
        rows = pl.ds(i * step, step)
        loads.append(pltpu.make_async_copy(acts.at[0, rows], abuf.at[rows], load_sem.at[2 + 2 * i]))
        loads.append(pltpu.make_async_copy(grads.at[0, rows], gbuf.at[rows], load_sem.at[3 + 2 * i]))
    for load in loads:
        load.start()

    peers = [(8 * d, 0) for d in range(1, 4)]
    peers += [(d, 0) for d in (1, 2, 4, 6)]
    peers += [(0, 4 * d) for d in range(1, 4)]
    low, high = z == 0, z == 3
    edge = jnp.logical_or(low, high)
    on_edge = jnp.where(edge, 1, 0)
    across = (jnp.bitwise_xor(clip, 24), y * 4 + lax.rem(zh + jnp.where(high, 1, 3), 4))
    barrier = pltpu.get_barrier_semaphore()

    def tell(sem, device):
        pl.semaphore_signal(sem, inc=1, device_id=device, device_id_type=MESH)

    for bits in peers:
        tell(barrier, at(*bits))

    @pl.when(edge)
    def _():
        tell(barrier, across)

    place = lax.broadcasted_iota(jnp.int32, (IDS, 128), 0) * 128 + lax.broadcasted_iota(
        jnp.int32, (IDS, 128), 1
    )
    owner = jnp.zeros((IDS, 128), jnp.int32)
    end = jnp.int32(0)
    token_load.wait()
    for c in range(CLIPS - 1):
        end = end + counts[c]
        owner = owner + jnp.where(place >= end, 1, 0)
    blocks[0, ROWS:, :] = owner.astype(jnp.float32).astype(jnp.bfloat16)

    loads[0].wait()
    loads[1].wait()
    for i in range(PIECES):
        rows = pl.ds(i * step, step)
        loads[2 + 2 * i].wait()
        loads[3 + 2 * i].wait()
        v = dot_nt(abuf[rows, :], ibuf[...])
        u = dot_nt(gbuf[rows, :], obuf[...])
        blocks[0, rows, :] = jnp.concatenate([u, v], axis=1).astype(jnp.bfloat16)

    pl.semaphore_wait(barrier, len(peers) + on_edge)

    def send_block(src, slot, bits):
        copy = pltpu.make_async_remote_copy(
            src_ref=blocks.at[src], dst_ref=blocks.at[slot], send_sem=send1.at[slot],
            recv_sem=recv1.at[slot], device_id=at(bits, 0), device_id_type=MESH,
        )
        copy.start()
        return copy

    def column_send(n):
        return pltpu.make_async_remote_copy(
            src_ref=blocks.at[0], dst_ref=blocks.at[7 + gives[n]], send_sem=send1.at[8 + n],
            recv_sem=recv1.at[7 + gives[n]], device_id=at(8 * gives[n], 0), device_id_type=MESH,
        )

    sends = [send_block(0, 1, 1), send_block(0, 4, 4), send_block(0, 2, 2), send_block(0, 6, 6)]
    column_send(0).start()
    column_send(1).start()
    for d in range(1, 4):
        tell(plane_in, at(2 * d, 0))
        tell(run_in, at(8 * d, 0))

    @pl.when(edge)
    def _():
        tell(edge_in, across)

    def relay_one():
        @pl.when(edge)
        def _():
            pl.semaphore_wait(edge_in, 1)
            for d in range(1, 4):
                tell(next_in, at(8 * d, 0))

    def relay_two():
        pl.semaphore_wait(next_in, 2 - on_edge)

        @pl.when(high)
        def _():
            tell(edge_two, across)

    def relay_three():
        @pl.when(low)
        def _():
            pl.semaphore_wait(edge_two, 1)
            for d in range(1, 4):
                tell(two_in, at(8 * d, 0))

    def relay_four():
        @pl.when(jnp.logical_not(low))
        def _():
            pl.semaphore_wait(two_in, 1)

    def block_arrives(slot):
        pltpu.make_async_remote_copy(
            src_ref=blocks.at[0], dst_ref=blocks.at[slot], send_sem=send1.at[slot],
            recv_sem=recv1.at[slot], device_id=at(1, 0), device_id_type=MESH,
        ).wait_recv()

    lane = lax.broadcasted_iota(jnp.int32, (1, 128), 1)
    group = lane // CLIPS

    def by_group(pieces):
        out = pieces[0]
        for g in range(1, 4):
            out = jnp.where(group == g, pieces[g], out)
        return out

    def hot_ids(slot, which):
        ids = blocks[slot, ROWS:, :].astype(jnp.float32)
        halves = [jnp.where(which == ids[i : i + 1, :], 1.0, 0.0) for i in range(2)]
        return jnp.concatenate(halves, axis=1)

    def row_slot(kx, i):
        return 2 * kx + i

    def take_rows(kx):
        for i in range(2):
            slot = row_slot(kx, i)
            if i:
                block_arrives(slot)
            hot = hot_ids(slot, lax.broadcasted_iota(jnp.int32, (CLIPS, 128), 0).astype(jnp.float32))
            pool_r[kx, i] = hot.astype(jnp.bfloat16)
            scale = inverse_root(jnp.sum(hot, axis=1, keepdims=True))
            scale_r[kx, i] = by_group([scale[8 * g : 8 * g + 8] for g in range(4)])

    def take_cols(kz):
        slot = 0
        if kz:
            slot = 7 + takes[kz - 1]
            block_arrives(slot)
        cols = blocks[slot, pl.ds(0, ROWS), :]
        pairs[kz, 0:ROWS] = jnp.where(lane < WIDE, cols, jnp.zeros_like(cols))
        pairs[kz, ROWS:] = jnp.where(lane < WIDE, jnp.zeros_like(cols), cols)
        j = lax.broadcasted_iota(jnp.int32, (128, 128), 0)
        which = jnp.where((j // CLIPS) % 2 == kz % 2, j % CLIPS, -1).astype(jnp.float32)
        hot = hot_ids(slot, which).astype(jnp.bfloat16)
        pool_c[kz] = hot
        count = dot_nt(jnp.ones((16, ROWS), jnp.bfloat16), hot)[0:8]
        scale_c[kz] = inverse_root(count + pltpu.roll(count, CLIPS, 1))

    def to_near(kx, i, kz):
        bits = row_slot(kx, i)
        dy = jnp.bitwise_xor(apart, takes[kz - 1]) if kz else apart
        copy = pltpu.make_async_remote_copy(
            src_ref=part.at[kz, bits], dst_ref=near.at[dy, bits], send_sem=send2.at[kz * 8 + kx * 2 + i],
            recv_sem=recv2.at[dy * 8 + bits], device_id=at(bits, 4 * dy), device_id_type=MESH,
        )
        return dy * 8 + bits, copy

    def may_stay(kx, i):
        return i == 0 and not (isinstance(kx, int) and kx)

    def to_other_run(kz):
        here, there = part.at[kz], near.at[apart]
        if kz == 2:
            here, there = part.at[2, pl.ds(4 * odd, 4)], near.at[apart, pl.ds(4 * odd, 4)]
        return pltpu.make_async_remote_copy(
            src_ref=here, dst_ref=there, send_sem=send2.at[24 + kz],
            recv_sem=recv4.at[apart], device_id=at(8 * takes[kz - 1], 4 * apart), device_id_type=MESH,
        )

    def pooled_pairs(kx, kz):
        rows = [blocks[row_slot(kx, i), pl.ds(0, ROWS), :] for i in range(2)]
        gram = dot_nt(jnp.concatenate(rows, axis=0), pairs[kz])
        gram = (gram[:, 0:ROWS] * gram[:, ROWS:]).astype(jnp.bfloat16)
        return dot_nt(gram, pool_c[kz])

    def finish(kx, kzs, pooled):
        for i in range(2):
            tile = jnp.dot(
                pool_r[kx, i],
                pooled[i * ROWS : (i + 1) * ROWS].astype(jnp.bfloat16),
                preferred_element_type=jnp.float32,
            )
            moved = pltpu.roll(tile, CLIPS, 1)
            for n, k in enumerate(kzs):
                pieces = [(moved if (g + n) % 2 else tile)[8 * g : 8 * g + 8] for g in range(4)]
                part[k, row_slot(kx, i)] = by_group(pieces) * scale_r[kx, i] * scale_c[k]
                slot, copy = to_near(kx, i, k)
                if not may_stay(kx, i):
                    copy.start()
                else:

                    @pl.when(slot != 0)
                    def _():
                        copy.start()

                    @pl.when(slot == 0)
                    def _():
                        near[0, 0] = part[k, 0]

    take_cols(0)
    take_rows(0)
    held[0] = pooled_pairs(0, 0)
    relay_one()
    for kx in (1, 3, 2):
        slot = row_slot(kx, 0)
        block_arrives(slot)
        sends.append(send_block(slot, slot + 1, 1))
    pl.semaphore_wait(plane_in, 3)
    tell(other_in, at(1, 0))
    relay_two()
    take_cols(1)
    take_cols(2)
    pl.semaphore_wait(other_in, 1)
    for kx in (0, 1, 3, 2):
        if kx:
            take_rows(kx)
            held[kx] = pooled_pairs(kx, 0)
        finish(kx, (0, 1), held[kx] + pooled_pairs(kx, 1))
        if kx == 1:
            relay_three()
        if kx == 3:
            pl.semaphore_wait(run_in, 3)
    to_other_run(1).start()
    halves = [jnp.bitwise_xor(n, 3 * odd) for n in range(2)]
    for kx in halves:
        finish(kx, (2,), pooled_pairs(kx, 2))
    to_other_run(2).start()
    relay_four()

    def run_arrives(dy, there):
        pltpu.make_async_remote_copy(
            src_ref=there, dst_ref=there, send_sem=send2.at[25],
            recv_sem=recv4.at[dy], device_id=at(1, 0), device_id_type=MESH,
        ).wait_recv()

    @pl.when(apart == 1)
    def _():
        for dy in range(4):
            run_arrives(dy, near.at[dy, pl.ds(4 * (1 - odd), 4)])

    @pl.when(jnp.logical_not((apart == 0) | (apart == 1) | (apart == takes[0])))
    def _():
        for dy in range(4):
            run_arrives(dy, near.at[dy])

    def gathered(d, dc):
        dx = jnp.bitwise_xor(jnp.bitwise_xor(x, zh), d)
        bits = 2 * dx + dc
        total = jnp.zeros((8, 128), jnp.float32)
        for dy in range(4):
            slot = dy * 8 + bits
            arrival = pltpu.make_async_remote_copy(
                src_ref=part.at[0, 0], dst_ref=near.at[dy, bits], send_sem=send2.at[0],
                recv_sem=recv2.at[slot], device_id=at(1, 0), device_id_type=MESH,
            )

            @pl.when(straight_from(dx) & (slot != 0))
            def _():
                arrival.wait_recv()

            total = total + near[dy, bits]
        return total

    last = []
    for d in (2, 1, 3):
        for dc in range(2):
            half[d, dc] = gathered(d, dc)
        copy = pltpu.make_async_remote_copy(
            src_ref=half.at[d], dst_ref=far.at[d], send_sem=send3.at[d], recv_sem=recv3.at[d],
            device_id=at(0, d), device_id_type=MESH,
        )
        copy.start()
        last.append(copy)
    total = [gathered(0, dc) for dc in range(2)]
    for copy in last:
        copy.wait_recv()
    norm = 1.0 / math.sqrt(16 * WIDE * WIDE)
    mine = straight_from(jnp.bitwise_xor(x, zh))
    for side in range(2):
        here, there = (
            jnp.where(core == side, pair[0], pair[1]) * norm
            for pair in ([total[dc] + far[1, dc] for dc in range(2)], [far[2, dc] + far[3, dc] for dc in range(2)])
        )
        straight = jnp.where(mine, here, there) + jnp.where(apart == 0, there, 0.0)
        crossed = jnp.where(apart == 0, 0.0, jnp.where(mine, there, here))
        straight, crossed = (
            jnp.concatenate([packed[:, CLIPS * g : CLIPS * (g + 1)] for g in range(4)], axis=0)
            for packed in (straight, crossed)
        )
        crossed = jnp.concatenate([crossed, jnp.zeros((CLIPS, 128 - CLIPS), jnp.float32)], axis=1)
        crossed = jnp.concatenate([crossed, jnp.zeros((128 - CLIPS, 128), jnp.float32)], axis=0)
        out[:, CLIPS * side : CLIPS * (side + 1)] = straight + crossed.T[0:CLIPS, 0:CLIPS]

    for copy in sends:
        copy.wait_send()
    column_send(0).wait_send()

    column_send(1).wait_send()

    def near_sent(kx, kz):
        for i in range(2):
            slot, copy = to_near(kx, i, kz)
            if not may_stay(kx, i):
                copy.wait_send()
            else:

                @pl.when(slot != 0)
                def _():
                    copy.wait_send()

    for kx in range(4):
        for kz in range(2):
            near_sent(kx, kz)
    for kx in halves:
        near_sent(kx, 2)
    for kz in (1, 2):
        to_other_run(kz).wait_send()
    for copy in last:
        copy.wait_send()


def body(acts, grads, in_factor, out_factor, clip_tokens):
    depth = acts.shape[2]
    bf16, f32 = jnp.bfloat16, jnp.float32
    hbm = pl.BlockSpec(memory_space=pltpu.HBM)
    return pl.pallas_call(
        kernel,
        out_shape=pltpu.VMEM((CLIPS, 64), f32),
        in_specs=[hbm] * 4 + [hbm],
        out_specs=pl.BlockSpec(memory_space=pltpu.VMEM),
        scratch_shapes=[
            pltpu.VMEM((ROWS, depth), bf16),
            pltpu.VMEM((ROWS, depth), bf16),
            pltpu.VMEM((WIDE, depth), bf16),
            pltpu.VMEM((WIDE, depth), bf16),
            pltpu.VMEM((11, ROWS + IDS, 128), bf16),
            pltpu.VMEM((4, 2 * ROWS, 128), bf16),
            pltpu.VMEM((4, 2, CLIPS, ROWS), bf16),
            pltpu.VMEM((4, 128, ROWS), bf16),
            pltpu.VMEM((4, 2, 8, 128), f32),
            pltpu.VMEM((4, 8, 128), f32),
            pltpu.VMEM((4, 2 * ROWS, 128), f32),
            pltpu.VMEM((3, 8, 8, 128), f32),
            pltpu.VMEM((4, 8, 8, 128), f32),
            pltpu.VMEM((4, 2, 8, 128), f32),
            pltpu.VMEM((4, 2, 8, 128), f32),
            pltpu.SemaphoreType.DMA((2 + 2 * PIECES,)),
            pltpu.SemaphoreType.DMA((11,)),
            pltpu.SemaphoreType.DMA((11,)),
            pltpu.SemaphoreType.DMA((32,)),
            pltpu.SemaphoreType.DMA((32,)),
            pltpu.SemaphoreType.DMA((4,)),
            pltpu.SemaphoreType.DMA((4,)),
            pltpu.SemaphoreType.DMA((4,)),
        ]
        + [pltpu.SMEM((CLIPS,), jnp.int32), pltpu.SemaphoreType.DMA(())]
        + [pltpu.SemaphoreType.REGULAR] * 7,
        compiler_params=pltpu.CompilerParams(
            collective_id=0, has_side_effects=True, vmem_limit_bytes=60 * 1024 * 1024
        ),
        cost_estimate=pl.CostEstimate(flops=10**9, bytes_accessed=7 * 10**6, transcendentals=0),
        name="similarity",
    )(
        acts,
        grads,
        jnp.swapaxes(in_factor, 1, 2),
        jnp.swapaxes(out_factor, 1, 2),
        clip_tokens,
    )


def solution(mesh):
    return jax.shard_map(
        body,
        mesh=mesh,
        in_specs=(
            P("layer", "clip", None),
            P("layer", "clip", None),
            P("layer", None, None),
            P("layer", None, None),
            P("clip"),
        ),
        out_specs=P("clip", "layer"),
        check_vma=False,
    )
```

```python
import functools
import math

import jax
import jax.numpy as jnp
from jax import lax
from jax.experimental import pallas as pl
from jax.experimental.pallas import tpu as pltpu
from jax.sharding import PartitionSpec as P

MESH = pl.DeviceIdType.MESH
NT = (((1,), (1,)), ((), ()))
ROWS = 256
CLIPS = 32
WIDE = 64
IDS = 16
PIECES = 4


def dot_nt(a, b):
    return lax.dot_general(a, b, NT, preferred_element_type=jnp.float32)


def inverse_root(n):
    r = lax.rsqrt(n)
    return r * (1.5 - 0.5 * n * r * r)


def kernel(
    acts, grads, in_t, out_t, tokens, out,
    abuf, gbuf, ibuf, obuf, blocks, pairs, pool_r, pool_c, scale_r, scale_c,
    held, part, near, half, far,
    load_sem, send1, recv1, send2, recv2, send3, recv3, recv4,
    counts, counts_sem, plane_in, other_in, run_in, edge_in, next_in, edge_two, two_in,
):
    clip, layer = lax.axis_index("clip"), lax.axis_index("layer")
    z, x, core = clip // 8, (clip // 2) % 4, clip % 2
    y, zh = layer // 4, layer % 4

    turn = jnp.where(zh >= 2, z, 3 - z)
    odd = turn % 2
    takes = (jnp.where(turn < 2, 3, 2), 1)
    gives = (jnp.where(turn < 2, 2, 3), 1)
    apart = jnp.bitwise_xor(y, z)

    def straight_from(dx):
        half = (dx // 2) == odd
        return (apart == 0) | (apart == takes[0]) | ((apart == 1) & half)

    def at(clip_bits, layer_bits):
        return (jnp.bitwise_xor(clip, clip_bits), jnp.bitwise_xor(layer, layer_bits))

    token_load = pltpu.make_async_copy(tokens, counts, counts_sem)
    token_load.start()
    loads = [
        pltpu.make_async_copy(in_t.at[0], ibuf, load_sem.at[0]),
        pltpu.make_async_copy(out_t.at[0], obuf, load_sem.at[1]),
    ]
    step = ROWS // PIECES
    for i in range(PIECES):
        rows = pl.ds(i * step, step)
        loads.append(pltpu.make_async_copy(acts.at[0, rows], abuf.at[rows], load_sem.at[2 + 2 * i]))
        loads.append(pltpu.make_async_copy(grads.at[0, rows], gbuf.at[rows], load_sem.at[3 + 2 * i]))
    for load in loads:
        load.start()

    peers = [(8 * d, 0) for d in range(1, 4)]
    peers += [(d, 0) for d in (1, 2, 4, 6)]
    peers += [(0, 4 * d) for d in range(1, 4)]
    low, high = z == 0, z == 3
    edge = jnp.logical_or(low, high)
    on_edge = jnp.where(edge, 1, 0)
    across = (jnp.bitwise_xor(clip, 24), y * 4 + lax.rem(zh + jnp.where(high, 1, 3), 4))
    barrier = pltpu.get_barrier_semaphore()

    def tell(sem, device):
        pl.semaphore_signal(sem, inc=1, device_id=device, device_id_type=MESH)

    for bits in peers:
        tell(barrier, at(*bits))

    @pl.when(edge)
    def _():
        tell(barrier, across)

    place = lax.broadcasted_iota(jnp.int32, (IDS, 128), 0) * 128 + lax.broadcasted_iota(
        jnp.int32, (IDS, 128), 1
    )
    owner = jnp.zeros((IDS, 128), jnp.int32)
    end = jnp.int32(0)
    token_load.wait()
    for c in range(CLIPS - 1):
        end = end + counts[c]
        owner = owner + jnp.where(place >= end, 1, 0)
    blocks[0, ROWS:, :] = owner.astype(jnp.float32).astype(jnp.bfloat16)

    loads[0].wait()
    loads[1].wait()
    for i in range(PIECES):
        rows = pl.ds(i * step, step)
        loads[2 + 2 * i].wait()
        loads[3 + 2 * i].wait()
        v = dot_nt(abuf[rows, :], ibuf[...])
        u = dot_nt(gbuf[rows, :], obuf[...])
        blocks[0, rows, :] = jnp.concatenate([u, v], axis=1).astype(jnp.bfloat16)

    pl.semaphore_wait(barrier, len(peers) + on_edge)

    def send_block(src, slot, bits):
        copy = pltpu.make_async_remote_copy(
            src_ref=blocks.at[src], dst_ref=blocks.at[slot], send_sem=send1.at[slot],
            recv_sem=recv1.at[slot], device_id=at(bits, 0), device_id_type=MESH,
        )
        copy.start()
        return copy

    def column_send(n):
        return pltpu.make_async_remote_copy(
            src_ref=blocks.at[0], dst_ref=blocks.at[7 + gives[n]], send_sem=send1.at[8 + n],
            recv_sem=recv1.at[7 + gives[n]], device_id=at(8 * gives[n], 0), device_id_type=MESH,
        )

    sends = [send_block(0, 1, 1), send_block(0, 4, 4), send_block(0, 2, 2), send_block(0, 6, 6)]
    column_send(0).start()
    column_send(1).start()
    for d in range(1, 4):
        tell(plane_in, at(2 * d, 0))
        tell(run_in, at(8 * d, 0))

    @pl.when(edge)
    def _():
        tell(edge_in, across)

    def relay_one():
        @pl.when(edge)
        def _():
            pl.semaphore_wait(edge_in, 1)
            for d in range(1, 4):
                tell(next_in, at(8 * d, 0))

    def relay_two():
        pl.semaphore_wait(next_in, 2 - on_edge)

        @pl.when(high)
        def _():
            tell(edge_two, across)

    def relay_three():
        @pl.when(low)
        def _():
            pl.semaphore_wait(edge_two, 1)
            for d in range(1, 4):
                tell(two_in, at(8 * d, 0))

    def relay_four():
        @pl.when(jnp.logical_not(low))
        def _():
            pl.semaphore_wait(two_in, 1)

    def block_arrives(slot):
        pltpu.make_async_remote_copy(
            src_ref=blocks.at[0], dst_ref=blocks.at[slot], send_sem=send1.at[slot],
            recv_sem=recv1.at[slot], device_id=at(1, 0), device_id_type=MESH,
        ).wait_recv()

    lane = lax.broadcasted_iota(jnp.int32, (1, 128), 1)
    group = lane // CLIPS

    def by_group(pieces):
        out = pieces[0]
        for g in range(1, 4):
            out = jnp.where(group == g, pieces[g], out)
        return out

    def hot_ids(slot, which):
        ids = blocks[slot, ROWS:, :].astype(jnp.float32)
        halves = [jnp.where(which == ids[i : i + 1, :], 1.0, 0.0) for i in range(2)]
        return jnp.concatenate(halves, axis=1)

    def row_slot(kx, i):
        return 2 * kx + i

    def take_rows(kx):
        for i in range(2):
            slot = row_slot(kx, i)
            if i:
                block_arrives(slot)
            hot = hot_ids(slot, lax.broadcasted_iota(jnp.int32, (CLIPS, 128), 0).astype(jnp.float32))
            pool_r[kx, i] = hot.astype(jnp.bfloat16)
            scale = inverse_root(jnp.sum(hot, axis=1, keepdims=True))
            scale_r[kx, i] = by_group([scale[8 * g : 8 * g + 8] for g in range(4)])

    def take_cols(kz):
        slot = 0
        if kz:
            slot = 7 + takes[kz - 1]
            block_arrives(slot)
        cols = blocks[slot, pl.ds(0, ROWS), :]
        pairs[kz, 0:ROWS] = jnp.where(lane < WIDE, cols, jnp.zeros_like(cols))
        pairs[kz, ROWS:] = jnp.where(lane < WIDE, jnp.zeros_like(cols), cols)
        j = lax.broadcasted_iota(jnp.int32, (128, 128), 0)
        which = jnp.where((j // CLIPS) % 2 == kz % 2, j % CLIPS, -1).astype(jnp.float32)
        hot = hot_ids(slot, which).astype(jnp.bfloat16)
        pool_c[kz] = hot
        count = dot_nt(jnp.ones((16, ROWS), jnp.bfloat16), hot)[0:8]
        scale_c[kz] = inverse_root(count + pltpu.roll(count, CLIPS, 1))

    def to_near(kx, i, kz):
        bits = row_slot(kx, i)
        dy = jnp.bitwise_xor(apart, takes[kz - 1]) if kz else apart
        copy = pltpu.make_async_remote_copy(
            src_ref=part.at[kz, bits], dst_ref=near.at[dy, bits], send_sem=send2.at[kz * 8 + kx * 2 + i],
            recv_sem=recv2.at[bits // 2], device_id=at(bits, 4 * dy), device_id_type=MESH,
        )
        return dy * 8 + bits, copy

    def may_stay(kx, i):
        return i == 0 and not (isinstance(kx, int) and kx)

    def to_other_run(kz):
        here, there = part.at[kz], near.at[apart]
        if kz == 2:
            here, there = part.at[2, pl.ds(4 * odd, 4)], near.at[apart, pl.ds(4 * odd, 4)]
        return pltpu.make_async_remote_copy(
            src_ref=here, dst_ref=there, send_sem=send2.at[24 + kz],
            recv_sem=recv4, device_id=at(8 * takes[kz - 1], 4 * apart), device_id_type=MESH,
        )

    def pooled_pairs(kx, kz):
        rows = [blocks[row_slot(kx, i), pl.ds(0, ROWS), :] for i in range(2)]
        gram = dot_nt(jnp.concatenate(rows, axis=0), pairs[kz])
        gram = (gram[:, 0:ROWS] * gram[:, ROWS:]).astype(jnp.bfloat16)
        return dot_nt(gram, pool_c[kz])

    def finish(kx, kzs, pooled):
        for i in range(2):
            tile = jnp.dot(
                pool_r[kx, i],
                pooled[i * ROWS : (i + 1) * ROWS].astype(jnp.bfloat16),
                preferred_element_type=jnp.float32,
            )
            moved = pltpu.roll(tile, CLIPS, 1)
            for n, k in enumerate(kzs):
                pieces = [(moved if (g + n) % 2 else tile)[8 * g : 8 * g + 8] for g in range(4)]
                part[k, row_slot(kx, i)] = by_group(pieces) * scale_r[kx, i] * scale_c[k]
                slot, copy = to_near(kx, i, k)
                if not may_stay(kx, i):
                    copy.start()
                else:

                    @pl.when(slot != 0)
                    def _():
                        copy.start()

                    @pl.when(slot == 0)
                    def _():
                        pltpu.make_async_copy(part.at[k, 0], near.at[0, 0], recv2.at[0]).start()

    take_cols(0)
    take_rows(0)
    held[0] = pooled_pairs(0, 0)
    relay_one()
    for kx in (1, 3, 2):
        slot = row_slot(kx, 0)
        block_arrives(slot)
        sends.append(send_block(slot, slot + 1, 1))
    pl.semaphore_wait(plane_in, 3)
    tell(other_in, at(1, 0))
    relay_two()
    take_cols(1)
    take_cols(2)
    pl.semaphore_wait(other_in, 1)
    for kx in (0, 1, 3, 2):
        if kx:
            take_rows(kx)
            held[kx] = pooled_pairs(kx, 0)
        finish(kx, (0, 1), held[kx] + pooled_pairs(kx, 1))
        if kx == 1:
            relay_three()
        if kx == 3:
            pl.semaphore_wait(run_in, 3)
    to_other_run(1).start()
    halves = [jnp.bitwise_xor(n, 3 * odd) for n in range(2)]
    for kx in halves:
        finish(kx, (2,), pooled_pairs(kx, 2))
    to_other_run(2).start()
    relay_four()

    def run_arrives(there):
        pltpu.make_async_remote_copy(
            src_ref=there, dst_ref=there, send_sem=send2.at[25],
            recv_sem=recv4, device_id=at(1, 0), device_id_type=MESH,
        ).wait_recv()

    @pl.when(apart == 1)
    def _():
        run_arrives(near.at[:, pl.ds(4 * (1 - odd), 4)])

    @pl.when(jnp.logical_not((apart == 0) | (apart == 1) | (apart == takes[0])))
    def _():
        run_arrives(near)

    def gathered(d):
        dx = jnp.bitwise_xor(jnp.bitwise_xor(x, zh), d)
        both = pl.ds(2 * dx, 2)

        @pl.when(straight_from(dx))
        def _():
            pltpu.make_async_remote_copy(
                src_ref=near.at[:, both], dst_ref=near.at[:, both], send_sem=send2.at[0],
                recv_sem=recv2.at[dx], device_id=at(1, 0), device_id_type=MESH,
            ).wait_recv()

        return near[0, both] + near[1, both] + near[2, both] + near[3, both]

    last = []
    for d in (2, 1, 3):
        half[d] = gathered(d)
        copy = pltpu.make_async_remote_copy(
            src_ref=half.at[d], dst_ref=far.at[d], send_sem=send3.at[d], recv_sem=recv3.at[d],
            device_id=at(0, d), device_id_type=MESH,
        )
        copy.start()
        last.append(copy)
    total = gathered(0)
    for copy in sends:
        copy.wait_send()
    column_send(0).wait_send()

    column_send(1).wait_send()

    def near_sent(kx, kz):
        for i in range(2):
            slot, copy = to_near(kx, i, kz)
            if not may_stay(kx, i):
                copy.wait_send()
            else:

                @pl.when(slot != 0)
                def _():
                    copy.wait_send()

    for kx in range(4):
        for kz in range(2):
            near_sent(kx, kz)
    for kx in halves:
        near_sent(kx, 2)
    for kz in (1, 2):
        to_other_run(kz).wait_send()
    for copy in last:
        copy.wait_send()

    for copy in last:
        copy.wait_recv()
    norm = 1.0 / math.sqrt(16 * WIDE * WIDE)
    mine = straight_from(jnp.bitwise_xor(x, zh))
    for side in range(2):
        here, there = (
            jnp.where(core == side, pair[0], pair[1]) * norm
            for pair in ([total[dc] + far[1, dc] for dc in range(2)], [far[2, dc] + far[3, dc] for dc in range(2)])
        )
        straight = jnp.where(mine, here, there) + jnp.where(apart == 0, there, 0.0)
        crossed = jnp.where(apart == 0, 0.0, jnp.where(mine, there, here))
        straight, crossed = (
            jnp.concatenate([packed[:, CLIPS * g : CLIPS * (g + 1)] for g in range(4)], axis=0)
            for packed in (straight, crossed)
        )
        crossed = jnp.concatenate([crossed, jnp.zeros((CLIPS, 128 - CLIPS), jnp.float32)], axis=1)
        crossed = jnp.concatenate([crossed, jnp.zeros((128 - CLIPS, 128), jnp.float32)], axis=0)
        out[:, CLIPS * side : CLIPS * (side + 1)] = straight + crossed.T[0:CLIPS, 0:CLIPS]


def body(acts, grads, in_factor, out_factor, clip_tokens):
    depth = acts.shape[2]
    bf16, f32 = jnp.bfloat16, jnp.float32
    hbm = pl.BlockSpec(memory_space=pltpu.HBM)
    return pl.pallas_call(
        kernel,
        out_shape=pltpu.VMEM((CLIPS, 64), f32),
        in_specs=[hbm] * 4 + [hbm],
        out_specs=pl.BlockSpec(memory_space=pltpu.VMEM),
        scratch_shapes=[
            pltpu.VMEM((ROWS, depth), bf16),
            pltpu.VMEM((ROWS, depth), bf16),
            pltpu.VMEM((WIDE, depth), bf16),
            pltpu.VMEM((WIDE, depth), bf16),
            pltpu.VMEM((11, ROWS + IDS, 128), bf16),
            pltpu.VMEM((4, 2 * ROWS, 128), bf16),
            pltpu.VMEM((4, 2, CLIPS, ROWS), bf16),
            pltpu.VMEM((4, 128, ROWS), bf16),
            pltpu.VMEM((4, 2, 8, 128), f32),
            pltpu.VMEM((4, 8, 128), f32),
            pltpu.VMEM((4, 2 * ROWS, 128), f32),
            pltpu.VMEM((3, 8, 8, 128), f32),
            pltpu.VMEM((4, 8, 8, 128), f32),
            pltpu.VMEM((4, 2, 8, 128), f32),
            pltpu.VMEM((4, 2, 8, 128), f32),
            pltpu.SemaphoreType.DMA((2 + 2 * PIECES,)),
            pltpu.SemaphoreType.DMA((11,)),
            pltpu.SemaphoreType.DMA((11,)),
            pltpu.SemaphoreType.DMA((32,)),
            pltpu.SemaphoreType.DMA((4,)),
            pltpu.SemaphoreType.DMA((4,)),
            pltpu.SemaphoreType.DMA((4,)),
            pltpu.SemaphoreType.DMA(()),
        ]
        + [pltpu.SMEM((CLIPS,), jnp.int32), pltpu.SemaphoreType.DMA(())]
        + [pltpu.SemaphoreType.REGULAR] * 7,
        compiler_params=pltpu.CompilerParams(
            collective_id=0, has_side_effects=True, vmem_limit_bytes=60 * 1024 * 1024
        ),
        cost_estimate=pl.CostEstimate(flops=10**9, bytes_accessed=7 * 10**6, transcendentals=0),
        name="similarity",
    )(
        acts,
        grads,
        jnp.swapaxes(in_factor, 1, 2),
        jnp.swapaxes(out_factor, 1, 2),
        clip_tokens,
    )


def solution(mesh):
    return jax.shard_map(
        body,
        mesh=mesh,
        in_specs=(
            P("layer", "clip", None),
            P("layer", "clip", None),
            P("layer", None, None),
            P("layer", None, None),
            P("clip"),
        ),
        out_specs=P("clip", "layer"),
        check_vma=False,
    )
```

```python
import functools
import math

import jax
import jax.numpy as jnp
from jax import lax
from jax.experimental import pallas as pl
from jax.experimental.pallas import tpu as pltpu
from jax.sharding import PartitionSpec as P

MESH = pl.DeviceIdType.MESH
NT = (((1,), (1,)), ((), ()))
ROWS = 256
CLIPS = 32
WIDE = 64
IDS = 16
PIECES = 4


def dot_nt(a, b):
    return lax.dot_general(a, b, NT, preferred_element_type=jnp.float32)


def inverse_root(n):
    r = lax.rsqrt(n)
    return r * (1.5 - 0.5 * n * r * r)


def kernel(
    acts, grads, in_t, out_t, tokens, out,
    abuf, gbuf, ibuf, obuf, blocks, pairs, pool_r, pool_c, scale_r, scale_c,
    held, part, near, half, far,
    load_sem, send1, recv1, send2, recv2, send3, recv3, recv4,
    counts, counts_sem, plane_in, other_in, run_in, edge_in, next_in, edge_two, two_in,
):
    clip, layer = lax.axis_index("clip"), lax.axis_index("layer")
    z, x, core = clip // 8, (clip // 2) % 4, clip % 2
    y, zh = layer // 4, layer % 4

    turn = jnp.where(zh >= 2, z, 3 - z)
    odd = turn % 2
    takes = (jnp.where(turn < 2, 3, 2), 1)
    gives = (jnp.where(turn < 2, 2, 3), 1)
    apart = jnp.bitwise_xor(y, z)

    def straight_from(dx):
        half = (dx // 2) == odd
        return (apart == 0) | (apart == takes[0]) | ((apart == 1) & half)

    def at(clip_bits, layer_bits):
        return (jnp.bitwise_xor(clip, clip_bits), jnp.bitwise_xor(layer, layer_bits))

    token_load = pltpu.make_async_copy(tokens, counts, counts_sem)
    token_load.start()
    loads = [
        pltpu.make_async_copy(in_t.at[0], ibuf, load_sem.at[0]),
        pltpu.make_async_copy(out_t.at[0], obuf, load_sem.at[1]),
    ]
    step = ROWS // PIECES
    for i in range(PIECES):
        rows = pl.ds(i * step, step)
        loads.append(pltpu.make_async_copy(acts.at[0, rows], abuf.at[rows], load_sem.at[2 + 2 * i]))
        loads.append(pltpu.make_async_copy(grads.at[0, rows], gbuf.at[rows], load_sem.at[3 + 2 * i]))
    for load in loads:
        load.start()

    peers = [(8 * d, 0) for d in range(1, 4)]
    peers += [(d, 0) for d in (1, 2, 4, 6)]
    peers += [(0, 4 * d) for d in range(1, 4)]
    low, high = z == 0, z == 3
    edge = jnp.logical_or(low, high)
    on_edge = jnp.where(edge, 1, 0)
    across = (jnp.bitwise_xor(clip, 24), y * 4 + lax.rem(zh + jnp.where(high, 1, 3), 4))
    barrier = pltpu.get_barrier_semaphore()

    def tell(sem, device):
        pl.semaphore_signal(sem, inc=1, device_id=device, device_id_type=MESH)

    for bits in peers:
        tell(barrier, at(*bits))

    @pl.when(edge)
    def _():
        tell(barrier, across)

    place = lax.broadcasted_iota(jnp.int32, (IDS, 128), 0) * 128 + lax.broadcasted_iota(
        jnp.int32, (IDS, 128), 1
    )
    owner = jnp.zeros((IDS, 128), jnp.int32)
    end = jnp.int32(0)
    token_load.wait()
    for c in range(CLIPS - 1):
        end = end + counts[c]
        owner = owner + jnp.where(place >= end, 1, 0)
    blocks[0, ROWS:, :] = owner.astype(jnp.float32).astype(jnp.bfloat16)

    loads[0].wait()
    loads[1].wait()
    for i in range(PIECES):
        rows = pl.ds(i * step, step)
        loads[2 + 2 * i].wait()
        loads[3 + 2 * i].wait()
        v = dot_nt(abuf[rows, :], ibuf[...])
        u = dot_nt(gbuf[rows, :], obuf[...])
        blocks[0, rows, :] = jnp.concatenate([u, v], axis=1).astype(jnp.bfloat16)

    pl.semaphore_wait(barrier, len(peers) + on_edge)

    def send_block(src, slot, bits):
        copy = pltpu.make_async_remote_copy(
            src_ref=blocks.at[src], dst_ref=blocks.at[slot], send_sem=send1.at[slot],
            recv_sem=recv1.at[slot], device_id=at(bits, 0), device_id_type=MESH,
        )
        copy.start()
        return copy

    def column_send(n):
        return pltpu.make_async_remote_copy(
            src_ref=blocks.at[0], dst_ref=blocks.at[7 + gives[n]], send_sem=send1.at[8 + n],
            recv_sem=recv1.at[7 + gives[n]], device_id=at(8 * gives[n], 0), device_id_type=MESH,
        )

    sends = [send_block(0, 1, 1), send_block(0, 4, 4), send_block(0, 2, 2), send_block(0, 6, 6)]
    column_send(0).start()
    column_send(1).start()
    for d in range(1, 4):
        tell(plane_in, at(2 * d, 0))
        tell(run_in, at(8 * d, 0))

    @pl.when(edge)
    def _():
        tell(edge_in, across)

    def relay_one():
        @pl.when(edge)
        def _():
            pl.semaphore_wait(edge_in, 1)
            for d in range(1, 4):
                tell(next_in, at(8 * d, 0))

    def relay_two():
        pl.semaphore_wait(next_in, 2 - on_edge)

        @pl.when(high)
        def _():
            tell(edge_two, across)

    def relay_three():
        @pl.when(low)
        def _():
            pl.semaphore_wait(edge_two, 1)
            for d in range(1, 4):
                tell(two_in, at(8 * d, 0))

    def relay_four():
        @pl.when(jnp.logical_not(low))
        def _():
            pl.semaphore_wait(two_in, 1)

    def block_arrives(slot):
        pltpu.make_async_remote_copy(
            src_ref=blocks.at[0], dst_ref=blocks.at[slot], send_sem=send1.at[slot],
            recv_sem=recv1.at[slot], device_id=at(1, 0), device_id_type=MESH,
        ).wait_recv()

    lane = lax.broadcasted_iota(jnp.int32, (1, 128), 1)
    group = lane // CLIPS

    def by_group(pieces):
        out = pieces[0]
        for g in range(1, 4):
            out = jnp.where(group == g, pieces[g], out)
        return out

    def hot_ids(slot, which):
        ids = blocks[slot, ROWS:, :].astype(jnp.float32)
        halves = [jnp.where(which == ids[i : i + 1, :], 1.0, 0.0) for i in range(2)]
        return jnp.concatenate(halves, axis=1)

    def row_slot(kx, i):
        return 2 * kx + i

    def take_rows(kx):
        for i in range(2):
            slot = row_slot(kx, i)
            if i and not kx:
                block_arrives(slot)
            hot = hot_ids(slot, lax.broadcasted_iota(jnp.int32, (CLIPS, 128), 0).astype(jnp.float32))
            pool_r[kx, i] = hot.astype(jnp.bfloat16)
            scale = inverse_root(jnp.sum(hot, axis=1, keepdims=True))
            scale_r[kx, i] = by_group([scale[8 * g : 8 * g + 8] for g in range(4)])

    def take_cols(kz):
        slot = 0
        if kz:
            slot = 7 + takes[kz - 1]
            block_arrives(slot)
        cols = blocks[slot, pl.ds(0, ROWS), :]
        pairs[kz, 0:ROWS] = jnp.where(lane < WIDE, cols, jnp.zeros_like(cols))
        pairs[kz, ROWS:] = jnp.where(lane < WIDE, jnp.zeros_like(cols), cols)
        j = lax.broadcasted_iota(jnp.int32, (128, 128), 0)
        which = jnp.where((j // CLIPS) % 2 == kz % 2, j % CLIPS, -1).astype(jnp.float32)
        hot = hot_ids(slot, which).astype(jnp.bfloat16)
        pool_c[kz] = hot
        count = dot_nt(jnp.ones((16, ROWS), jnp.bfloat16), hot)[0:8]
        scale_c[kz] = inverse_root(count + pltpu.roll(count, CLIPS, 1))

    def to_near(kx, i, kz):
        bits = row_slot(kx, i)
        dy = jnp.bitwise_xor(apart, takes[kz - 1]) if kz else apart
        copy = pltpu.make_async_remote_copy(
            src_ref=part.at[kz, bits], dst_ref=near.at[dy, bits], send_sem=send2.at[kz * 8 + kx * 2 + i],
            recv_sem=recv2.at[bits // 2], device_id=at(bits, 4 * dy), device_id_type=MESH,
        )
        return dy * 8 + bits, copy

    def may_stay(kx, i):
        return i == 0 and not (isinstance(kx, int) and kx)

    def to_other_run(kz):
        here, there = part.at[kz], near.at[apart]
        if kz == 2:
            here, there = part.at[2, pl.ds(4 * odd, 4)], near.at[apart, pl.ds(4 * odd, 4)]
        return pltpu.make_async_remote_copy(
            src_ref=here, dst_ref=there, send_sem=send2.at[24 + kz],
            recv_sem=recv4, device_id=at(8 * takes[kz - 1], 4 * apart), device_id_type=MESH,
        )

    def pooled_pairs(kx, kz):
        rows = [blocks[row_slot(kx, i), pl.ds(0, ROWS), :] for i in range(2)]
        gram = dot_nt(jnp.concatenate(rows, axis=0), pairs[kz])
        gram = (gram[:, 0:ROWS] * gram[:, ROWS:]).astype(jnp.bfloat16)
        return dot_nt(gram, pool_c[kz])

    def finish(kx, kzs, pooled):
        for i in range(2):
            tile = jnp.dot(
                pool_r[kx, i],
                pooled[i * ROWS : (i + 1) * ROWS].astype(jnp.bfloat16),
                preferred_element_type=jnp.float32,
            )
            moved = pltpu.roll(tile, CLIPS, 1)
            for n, k in enumerate(kzs):
                pieces = [(moved if (g + n) % 2 else tile)[8 * g : 8 * g + 8] for g in range(4)]
                part[k, row_slot(kx, i)] = by_group(pieces) * scale_r[kx, i] * scale_c[k]
                slot, copy = to_near(kx, i, k)
                if not may_stay(kx, i):
                    copy.start()
                else:

                    @pl.when(slot != 0)
                    def _():
                        copy.start()

                    @pl.when(slot == 0)
                    def _():
                        pltpu.make_async_copy(part.at[k, 0], near.at[0, 0], recv2.at[0]).start()

    take_cols(0)
    take_rows(0)
    held[0] = pooled_pairs(0, 0)
    relay_one()
    for kx in (1, 3, 2):
        slot = row_slot(kx, 0)
        block_arrives(slot)
        sends.append(send_block(slot, slot + 1, 1))
    pl.semaphore_wait(plane_in, 3)
    tell(other_in, at(1, 0))
    relay_two()
    take_cols(1)
    take_cols(2)
    pl.semaphore_wait(other_in, 1)
    for kx in (0, 1, 3, 2):
        if kx:
            block_arrives(row_slot(kx, 1))
            held[kx] = pooled_pairs(kx, 0)
            take_rows(kx)
        finish(kx, (0, 1), held[kx] + pooled_pairs(kx, 1))
        if kx == 1:
            relay_three()
        if kx == 3:
            pl.semaphore_wait(run_in, 3)
    to_other_run(1).start()
    halves = [jnp.bitwise_xor(n, 3 * odd) for n in range(2)]
    for kx in halves:
        finish(kx, (2,), pooled_pairs(kx, 2))
    to_other_run(2).start()
    relay_four()

    def run_arrives(there):
        pltpu.make_async_remote_copy(
            src_ref=there, dst_ref=there, send_sem=send2.at[25],
            recv_sem=recv4, device_id=at(1, 0), device_id_type=MESH,
        ).wait_recv()

    @pl.when(apart == 1)
    def _():
        run_arrives(near.at[:, pl.ds(4 * (1 - odd), 4)])

    @pl.when(jnp.logical_not((apart == 0) | (apart == 1) | (apart == takes[0])))
    def _():
        run_arrives(near)

    def gathered(d):
        dx = jnp.bitwise_xor(jnp.bitwise_xor(x, zh), d)
        both = pl.ds(2 * dx, 2)

        @pl.when(straight_from(dx))
        def _():
            pltpu.make_async_remote_copy(
                src_ref=near.at[:, both], dst_ref=near.at[:, both], send_sem=send2.at[0],
                recv_sem=recv2.at[dx], device_id=at(1, 0), device_id_type=MESH,
            ).wait_recv()

        return near[0, both] + near[1, both] + near[2, both] + near[3, both]

    last = []
    for d in (2, 1, 3):
        half[d] = gathered(d)
        copy = pltpu.make_async_remote_copy(
            src_ref=half.at[d], dst_ref=far.at[d], send_sem=send3.at[d], recv_sem=recv3.at[d],
            device_id=at(0, d), device_id_type=MESH,
        )
        copy.start()
        last.append(copy)
    total = gathered(0)
    for copy in sends:
        copy.wait_send()
    column_send(0).wait_send()

    column_send(1).wait_send()

    def near_sent(kx, kz):
        for i in range(2):
            slot, copy = to_near(kx, i, kz)
            if not may_stay(kx, i):
                copy.wait_send()
            else:

                @pl.when(slot != 0)
                def _():
                    copy.wait_send()

    for kx in range(4):
        for kz in range(2):
            near_sent(kx, kz)
    for kx in halves:
        near_sent(kx, 2)
    for kz in (1, 2):
        to_other_run(kz).wait_send()
    for copy in last:
        copy.wait_send()

    for copy in last:
        copy.wait_recv()
    norm = 1.0 / math.sqrt(16 * WIDE * WIDE)
    mine = straight_from(jnp.bitwise_xor(x, zh))
    for side in range(2):
        here, there = (
            jnp.where(core == side, pair[0], pair[1]) * norm
            for pair in ([total[dc] + far[1, dc] for dc in range(2)], [far[2, dc] + far[3, dc] for dc in range(2)])
        )
        straight = jnp.where(mine, here, there) + jnp.where(apart == 0, there, 0.0)
        crossed = jnp.where(apart == 0, 0.0, jnp.where(mine, there, here))
        straight, crossed = (
            jnp.concatenate([packed[:, CLIPS * g : CLIPS * (g + 1)] for g in range(4)], axis=0)
            for packed in (straight, crossed)
        )
        crossed = jnp.concatenate([crossed, jnp.zeros((CLIPS, 128 - CLIPS), jnp.float32)], axis=1)
        crossed = jnp.concatenate([crossed, jnp.zeros((128 - CLIPS, 128), jnp.float32)], axis=0)
        out[:, CLIPS * side : CLIPS * (side + 1)] = straight + crossed.T[0:CLIPS, 0:CLIPS]


def body(acts, grads, in_factor, out_factor, clip_tokens):
    depth = acts.shape[2]
    bf16, f32 = jnp.bfloat16, jnp.float32
    hbm = pl.BlockSpec(memory_space=pltpu.HBM)
    return pl.pallas_call(
        kernel,
        out_shape=pltpu.VMEM((CLIPS, 64), f32),
        in_specs=[hbm] * 4 + [hbm],
        out_specs=pl.BlockSpec(memory_space=pltpu.VMEM),
        scratch_shapes=[
            pltpu.VMEM((ROWS, depth), bf16),
            pltpu.VMEM((ROWS, depth), bf16),
            pltpu.VMEM((WIDE, depth), bf16),
            pltpu.VMEM((WIDE, depth), bf16),
            pltpu.VMEM((11, ROWS + IDS, 128), bf16),
            pltpu.VMEM((4, 2 * ROWS, 128), bf16),
            pltpu.VMEM((4, 2, CLIPS, ROWS), bf16),
            pltpu.VMEM((4, 128, ROWS), bf16),
            pltpu.VMEM((4, 2, 8, 128), f32),
            pltpu.VMEM((4, 8, 128), f32),
            pltpu.VMEM((4, 2 * ROWS, 128), f32),
            pltpu.VMEM((3, 8, 8, 128), f32),
            pltpu.VMEM((4, 8, 8, 128), f32),
            pltpu.VMEM((4, 2, 8, 128), f32),
            pltpu.VMEM((4, 2, 8, 128), f32),
            pltpu.SemaphoreType.DMA((2 + 2 * PIECES,)),
            pltpu.SemaphoreType.DMA((11,)),
            pltpu.SemaphoreType.DMA((11,)),
            pltpu.SemaphoreType.DMA((32,)),
            pltpu.SemaphoreType.DMA((4,)),
            pltpu.SemaphoreType.DMA((4,)),
            pltpu.SemaphoreType.DMA((4,)),
            pltpu.SemaphoreType.DMA(()),
        ]
        + [pltpu.SMEM((CLIPS,), jnp.int32), pltpu.SemaphoreType.DMA(())]
        + [pltpu.SemaphoreType.REGULAR] * 7,
        compiler_params=pltpu.CompilerParams(
            collective_id=0, has_side_effects=True, vmem_limit_bytes=60 * 1024 * 1024
        ),
        cost_estimate=pl.CostEstimate(flops=10**9, bytes_accessed=7 * 10**6, transcendentals=0),
        name="similarity",
    )(
        acts,
        grads,
        jnp.swapaxes(in_factor, 1, 2),
        jnp.swapaxes(out_factor, 1, 2),
        clip_tokens,
    )


def solution(mesh):
    return jax.shard_map(
        body,
        mesh=mesh,
        in_specs=(
            P("layer", "clip", None),
            P("layer", "clip", None),
            P("layer", None, None),
            P("layer", None, None),
            P("clip"),
        ),
        out_specs=P("clip", "layer"),
        check_vma=False,
    )
```
